512 devices in a mesh: view: 32 (over x, z_hi, core), seq: 16 (over y, z_lo).
Axes of the slice: x: 4, y: 4, z: 16 (z_hi: 4, z_lo: 4; z = z_hi * 4 + z_lo), core: 2. Of those that a mesh axis runs over, the one named last changes fastest.
Arguments:
- query_rows: bfloat16 [32, 2048, 768], P('view', 'seq'), may hold values from -162 to 162
- key_rows: bfloat16 [32, 2048, 768], P('view', 'seq'), may hold values from -4.5 to 4.5
- value_rows: bfloat16 [32, 2048, 768], P('view', 'seq'), may hold values from -6 to 6
- head_gate: float32 [12], replicated, may hold values from 0.5 to 2
- cotangent: bfloat16 [32, 2048, 768], P('view', 'seq'), may hold values from -80 to 80
- neighbours: int32 [32, 4], P('view'), may hold values from 0 to 31, as said below
- counts: int32 [32], P('view'), may hold values from 1 to 4, as said below
Outputs:
- output: bfloat16 [32, 2048, 768], P('view', 'seq')
- query_grad: bfloat16 [32, 2048, 768], P('view', 'seq')
- key_grad: bfloat16 [32, 2048, 768], P('view', 'seq')
- value_grad: bfloat16 [32, 2048, 768], P('view', 'seq')
- gate_grad: float32 [12], replicated
The draws below stay inside these ranges and needn't reach their ends.
Inputs may be any that keep to these rules, and one draw needn't show every extreme that they name: Row v holds the views v - 2, v - 1, v + 1, v + 2 modulo 32, each once; the first counts[v] of them are the neighbours of v. Neighbourship is symmetric. `counts`: every view has a neighbour at distance one; some view has four neighbours.
All inputs are finite; a program needn't handle non-finite values.
Results may differ from the reference program's by a relative error of at most 0.035.
Values may be sent and summed in bfloat16 or wider, within the bound.
A program may use at most 64 MiB of HBM per device.

```python
import math
import jax
import jax.numpy as jnp
from jax import lax

H = 12
HD = 64
BLOCK = 128
VIEWS = 32
TOKENS_V = 2048
N_SEQ = 16


def base_keys(key):
    return jnp.clip(jax.random.normal(key, (VIEWS, TOKENS_V, H * HD), jnp.float32), -4.5, 4.5)


def cycle_links(key):
    bits = jax.random.randint(key, (3, VIEWS), 0, 2).astype(jnp.int32)
    bits = bits.at[0, VIEWS - 1].set(1).at[1, 0].set(1).at[2, VIEWS - 2].set(1)
    places = jnp.arange(VIEWS, dtype=jnp.int32)

    def odd_edge(lower):
        lower = lower % VIEWS
        return jnp.where(lower % 2 == 0, 1, bits[0, lower])

    def two_edge(lower):
        lower = lower % VIEWS
        return jnp.where(lower % 4 < 2, bits[1, lower], bits[2, lower])
    present = jnp.stack([two_edge(places - 2), odd_edge(places - 1), odd_edge(places), two_edge(places)], axis=1)
    offsets = jnp.array([-2, -1, 1, 2], dtype=jnp.int32)
    candidates = (places[:, None] + offsets[None, :]) % VIEWS
    slots = jnp.arange(4, dtype=jnp.int32)[None, :]
    order = jnp.argsort(jnp.where(present == 1, slots, slots + 4), axis=1, stable=True)
    listed = jnp.take_along_axis(candidates, order, axis=1).astype(jnp.int32)
    return (listed, jnp.sum(present, axis=1).astype(jnp.int32))


def draw_neighbours(key, part):
    listed, number = cycle_links(jax.random.fold_in(key, 21))
    return listed


def draw_counts(key, part):
    listed, number = cycle_links(jax.random.fold_in(key, 21))
    return number


def draw_key_rows(key, part):
    shared = base_keys(key)
    return shared.astype(jnp.bfloat16)


def draw_query_rows(key, part):
    key = jax.random.fold_in(key, 5)
    own_rows = jnp.clip(jax.random.normal(key, (VIEWS, TOKENS_V, H * HD), jnp.float32), -4.5, 4.5)
    return own_rows.astype(jnp.bfloat16)


def draw_cotangent(key, part):
    key = jax.random.fold_in(key, 11)
    first, second, third = jax.random.split(key, 3)
    total_rows = VIEWS * TOKENS_V
    ramp = (1.0 + 2.0 * jnp.arange(total_rows, dtype=jnp.float32) / (total_rows - 1)).reshape(VIEWS, TOKENS_V, 1)
    row_scale = jnp.exp((jax.random.uniform(second, (VIEWS, TOKENS_V, 1)) - 0.5) * math.log(3.3))
    col_scale = jnp.exp((jax.random.uniform(third, (1, 1, H * HD)) - 0.5) * math.log(10.0))
    base = jnp.clip(jax.random.normal(first, (VIEWS, TOKENS_V, H * HD), jnp.float32), -4.0, 4.0)
    return (base * ramp * row_scale * col_scale).astype(jnp.bfloat16)


def steps_of(rng, shape, cuts, low, high):
    def one(dim, shards_of):
        draws = jax.random.uniform(jax.random.fold_in(jax.random.fold_in(rng, 6), dim), (shards_of,), jnp.float32, low / len(cuts), high / len(cuts))
        return jnp.repeat(jnp.exp(draws), shape[dim] // shards_of).reshape((-1,) + (1,) * (len(shape) - dim - 1))

    factor_of = one(*cuts[0])
    for cut in cuts[1:]:
        factor_of = factor_of * one(*cut)
    return factor_of


def bell_draw(stream_key, dims, deviation, most, cuts=(), held_as=jnp.bfloat16):
    factor_of = steps_of(stream_key, dims, cuts, -0.22, 0.18) if cuts else 1.0
    drawn = jax.random.normal(stream_key, dims, jnp.float32) * deviation * factor_of
    return jnp.minimum(jnp.maximum(drawn, -most), most).astype(held_as)


def setup_inputs(seed: int = 0) -> dict:
    key_list = jax.random.split(jax.random.key(seed), 8)
    return {
        "query_rows": draw_query_rows(jax.random.fold_in(key_list[7], 71), 0),
        "key_rows": draw_key_rows(jax.random.fold_in(key_list[7], 71), 0),
        "value_rows": bell_draw(key_list[2], (VIEWS, TOKENS_V, H * HD), 1.0, 6.0, ((0, 32), (1, 16))),
        "head_gate": jnp.clip(jnp.exp(jax.random.uniform(key_list[3], (H,), jnp.float32, math.log(0.5), math.log(2.0))), 0.5, 2.0),
        "cotangent": draw_cotangent(jax.random.fold_in(key_list[7], 71), 0),
        "neighbours": draw_neighbours(jax.random.fold_in(key_list[7], 71), 0),
        "counts": draw_counts(jax.random.fold_in(key_list[7], 71), 0),
    }


def reference(query_rows, key_rows, value_rows, head_gate, cotangent, neighbours, counts):
    shaped = (VIEWS, N_SEQ, BLOCK, H, HD)
    queries = query_rows.reshape(shaped)
    keys_all = key_rows.reshape(shaped)
    values_all = value_rows.reshape(shaped)
    cot_all = cotangent.reshape(shaped)
    own_index = jnp.arange(VIEWS, dtype=jnp.int32)
    index_table = jnp.concatenate([own_index[:, None], neighbours.astype(jnp.int32)], axis=1)
    keep_table = jnp.concatenate([jnp.ones((VIEWS, 1), dtype=bool), jnp.arange(4)[None, :] < counts[:, None]], axis=1)
    score_scale = 1.0 / math.sqrt(HD)
    gate_b = head_gate[None, None, :, None]

    def one_view(carry, inputs):
        key_acc, value_acc, gate_acc = carry
        view_q, view_c, chosen, keep_row = inputs
        near_keys = jnp.take(keys_all, chosen, axis=0).astype(jnp.float32)
        near_values = jnp.take(values_all, chosen, axis=0).astype(jnp.float32)
        q_float = view_q.astype(jnp.float32)
        scores = jnp.einsum('nbhd,jnchd->nhbjc', q_float, near_keys) * score_scale
        scores = jnp.where(keep_row[None, None, None, :, None], scores, -jnp.inf)
        top = lax.optimization_barrier(jnp.max(scores, axis=(3, 4), keepdims=True))
        log_total = top + jnp.log(lax.optimization_barrier(jnp.sum(jnp.exp(scores - top), axis=(3, 4), keepdims=True)))
        probs = jnp.exp(scores - log_total)
        weights = probs.astype(jnp.bfloat16)
        attended = jnp.einsum('nhbjc,jnchd->nbhd', weights.astype(jnp.float32), near_values)
        out_view = (gate_b * attended).astype(jnp.bfloat16)
        attn_grad = (gate_b * view_c.astype(jnp.float32)).astype(jnp.bfloat16)
        grad_float = attn_grad.astype(jnp.float32)
        row_delta = jnp.transpose(lax.optimization_barrier(jnp.sum(grad_float * attended, axis=3)), (0, 2, 1))
        prob_grad = jnp.einsum('nbhd,jnchd->nhbjc', grad_float, near_values)
        score_grad = (probs * (prob_grad - row_delta[:, :, :, None, None]) * score_scale).astype(jnp.bfloat16)
        sg_float = score_grad.astype(jnp.float32)
        query_part = jnp.einsum('nhbjc,jnchd->nbhd', sg_float, near_keys).astype(jnp.bfloat16)
        key_part = jnp.einsum('nhbjc,nbhd->jnchd', sg_float, q_float)
        value_part = jnp.einsum('nhbjc,nbhd->jnchd', weights.astype(jnp.float32), grad_float)
        key_part = lax.optimization_barrier(key_part.astype(jnp.bfloat16)).astype(jnp.float32)
        value_part = lax.optimization_barrier(value_part.astype(jnp.bfloat16)).astype(jnp.float32)
        gate_part = lax.optimization_barrier(jnp.sum(view_c.astype(jnp.float32) * attended, axis=(0, 1, 3)))
        key_acc = key_acc.at[chosen].add(key_part)
        value_acc = value_acc.at[chosen].add(value_part)
        return ((key_acc, value_acc, gate_acc + gate_part), (out_view, query_part))
    start = (jnp.zeros(shaped, jnp.float32), jnp.zeros(shaped, jnp.float32), jnp.zeros((H,), jnp.float32))
    (key_acc, value_acc, gate_acc), (outs, query_parts) = lax.scan(one_view, start, (queries, cot_all, index_table, keep_table))
    flat = (VIEWS, TOKENS_V, H * HD)
    output = outs.reshape(flat)
    query_grad = query_parts.reshape(flat)
    key_grad = key_acc.astype(jnp.bfloat16).reshape(flat)
    value_grad = value_acc.astype(jnp.bfloat16).reshape(flat)
    gate_grad = gate_acc / math.sqrt(VIEWS * TOKENS_V * HD)
    return (output, query_grad, key_grad, value_grad, gate_grad)
```

```python
import functools
import math

import jax
import jax.numpy as jnp
from jax import lax
from jax.experimental import pallas as pl
from jax.experimental.pallas import tpu as pltpu
from jax.sharding import PartitionSpec as P

MESH = pl.DeviceIdType.MESH
LANES = 128
OFFSETS = (0, -2, -1, 1, 2)
FROM_LOW2, FROM_LOW1, FROM_HIGH1, FROM_HIGH2 = 1, 2, 3, 4


def sum_rounds(n_view, n_seq):
    rounds = []
    low = math.gcd(n_view, 8)
    rounds.append(("view", 1, low))
    rounds.append(("view", low, n_view // low))
    low = math.gcd(n_seq, 4)
    rounds.append(("seq", 1, low))
    rounds.append(("seq", low, n_seq // low))
    return [r for r in rounds if r[2] > 1]


def kernel(
    sizes,
    gate_s, neigh_s, counts_s, q_hbm, k_hbm, v_hbm, c_hbm,
    out_ref, dq_ref, dk_ref, dv_ref, gg_ref,
    kv, qg, cot, stats, gacc, gbuf,
    load_sem, kv_send, kv_recv, qg_send, qg_recv, st_send, st_recv, g_send, g_recv,
):
    n_view, n_seq, pairs, head_size = sizes
    tokens = kv.shape[3]
    scale = 1.0 / math.sqrt(head_size)
    me = lax.axis_index("view")
    me_seq = lax.axis_index("seq")
    core = lax.rem(me, 2)
    sibling = me + 1 - 2 * core
    rounds = sum_rounds(n_view, n_seq)

    def view_at(offset):
        return lax.rem(me + offset + n_view, n_view)

    def partner(round_index, step):
        axis, stride, size = rounds[round_index]
        index = me if axis == "view" else me_seq
        digit = lax.rem(index // stride, size)
        other = lax.rem(digit + step, size)
        return {axis: index + (other - digit) * stride}, digit, other

    def load(hbm, column, p, dst):
        return pltpu.make_async_copy(
            hbm.at[0, :, pl.ds(p * LANES, LANES)], dst, load_sem.at[p, column]
        )

    loads = []
    for p in range(pairs):
        loads.append(
            [
                load(k_hbm, 0, p, kv.at[p, 0, 0]),
                load(v_hbm, 1, p, kv.at[p, 0, 1]),
                load(q_hbm, 2, p, qg.at[p, 0, 0]),
                load(c_hbm, 3, p, cot.at[p]),
            ]
        )
    for column in range(4):
        for p in range(pairs):
            loads[p][column].start()

    barrier = pltpu.get_barrier_semaphore()
    greeted = 0
    for offset in OFFSETS[1:]:
        pl.semaphore_signal(
            barrier, inc=1, device_id={"view": view_at(offset)}, device_id_type=MESH
        )
        greeted += 1
    for r in range(len(rounds)):
        for step in range(1, rounds[r][2]):
            pl.semaphore_signal(
                barrier, inc=1, device_id=partner(r, step)[0], device_id_type=MESH
            )
            greeted += 1
    pl.semaphore_wait(barrier, greeted)

    def block_copy(buf, send, recv, p, index):
        src_slot, dst_slot, target = (
            (0, FROM_LOW2, view_at(2)),
            (0, FROM_HIGH2, view_at(-2)),
            (0, 2 + core, sibling),
            (4 - 3 * core, 3 - core, sibling),
        )[index]
        return pltpu.make_async_remote_copy(
            src_ref=buf.at[p, src_slot],
            dst_ref=buf.at[p, dst_slot],
            send_sem=send.at[p, index],
            recv_sem=recv.at[p, dst_slot],
            device_id={"view": target},
            device_id_type=MESH,
        )

    def arrived(buf, send, recv, p, slot):
        pltpu.make_async_remote_copy(
            src_ref=buf.at[p, 0],
            dst_ref=buf.at[p, slot],
            send_sem=send.at[p, 0],
            recv_sem=recv.at[p, slot],
            device_id={"view": sibling},
            device_id_type=MESH,
        ).wait_recv()

    def stat_copy(p, slot):
        return pltpu.make_async_remote_copy(
            src_ref=stats.at[p, 0],
            dst_ref=stats.at[p, 5 - slot],
            send_sem=st_send.at[p, slot],
            recv_sem=st_recv.at[p, 5 - slot],
            device_id={"view": view_at(OFFSETS[slot])},
            device_id_type=MESH,
        )

    for p in range(pairs):
        loads[p][0].wait()
        loads[p][1].wait()
        for index in range(3):
            block_copy(kv, kv_send, kv_recv, p, index).start()
    for p in range(pairs):
        loads[p][2].wait()
        loads[p][3].wait()

    bias = [jnp.float32(0.0)]
    for offset in OFFSETS[1:]:
        view = view_at(offset)
        present = (neigh_s[0, 0] == view) & (counts_s[0] > 0)
        for j in range(1, 4):
            present = present | ((neigh_s[0, j] == view) & (counts_s[0] > j))
        bias.append(jnp.where(present, jnp.float32(0.0), jnp.float32(-jnp.inf)))
    bias_row = jnp.concatenate([jnp.full((1, tokens), b, jnp.float32) for b in bias], axis=1)
    lane = lax.broadcasted_iota(jnp.int32, (tokens, LANES), 1)
    low_half = lane < head_size

    def stacked(block):
        zero = jnp.zeros_like(block)
        return jnp.concatenate(
            [jnp.where(low_half, block, zero), jnp.where(low_half, zero, block)], axis=0
        )

    def unstacked(block):
        return jnp.where(low_half, block[:tokens], block[tokens:])

    def dot_t(a, b):
        return lax.dot_general(
            a, b, (((1,), (1,)), ((), ())), preferred_element_type=jnp.float32
        )

    def dot(a, b):
        return jnp.dot(a, b, preferred_element_type=jnp.float32)

    gacc[...] = jnp.zeros_like(gacc)

    def query_side(p):
        columns = pl.ds(pl.multiple_of(p * LANES, LANES), LANES)
        gate_row = jnp.where(low_half[:1], gate_s[2 * p], gate_s[2 * p + 1])
        cot_block = cot[p].astype(jnp.float32)
        grad = (gate_row * cot_block).astype(jnp.bfloat16)
        qg[p, 0, 1] = grad
        keys = kv[p, :, 0].reshape(5 * tokens, LANES)
        values = kv[p, :, 1].reshape(5 * tokens, LANES)
        scores = dot_t(stacked(qg[p, 0, 0]), keys) * scale + bias_row
        top = jnp.max(scores, axis=1, keepdims=True)
        raised = jnp.exp(scores - top)
        total = jnp.sum(raised, axis=1, keepdims=True)
        probs = raised * (1.0 / total)
        log_total = top + jnp.log(total)
        attended = unstacked(dot(probs.astype(jnp.bfloat16), values))
        out_ref[0, :, columns] = (gate_row * attended).astype(jnp.bfloat16)
        gacc[pl.ds(p, 1), :] = jnp.sum(cot_block * attended, axis=0, keepdims=True)
        product = grad.astype(jnp.float32) * attended
        delta_low = jnp.sum(jnp.where(low_half, product, 0.0), axis=1, keepdims=True)
        delta_high = jnp.sum(jnp.where(low_half, 0.0, product), axis=1, keepdims=True)
        table = jnp.where(lane == 0, log_total[:tokens], log_total[tokens:])
        table = jnp.where(lane == 2, delta_low, table)
        table = jnp.where(lane == 3, delta_high, table)
        stats[p, 0] = jnp.transpose(table)[:8]
        for slot in range(1, 5):
            stat_copy(p, slot).start()
        for index in range(3):
            block_copy(qg, qg_send, qg_recv, p, index).start()
        prob_grad = dot_t(stacked(grad), values)
        delta = jnp.concatenate([delta_low, delta_high], axis=0)
        score_grad = (probs * (prob_grad - delta) * scale).astype(jnp.bfloat16)
        dq_ref[0, :, columns] = unstacked(dot(score_grad, keys)).astype(jnp.bfloat16)

    def key_side(p):
        columns = pl.ds(pl.multiple_of(p * LANES, LANES), LANES)
        queries = qg[p, :, 0].reshape(5 * tokens, LANES)
        grads = qg[p, :, 1].reshape(5 * tokens, LANES)
        tables = [stats[p, slot] for slot in range(5)]
        rows = jnp.concatenate(tables, axis=1)

        def both(first, second):
            shape = (tokens, 5 * tokens)
            return jnp.concatenate(
                [jnp.broadcast_to(first, shape), jnp.broadcast_to(second, shape)], axis=0
            )

        log_total = both(rows[0:1] - bias_row, rows[1:2] - bias_row)
        delta = both(rows[2:3], rows[3:4])
        scores = dot_t(stacked(kv[p, 0, 0]), queries) * scale
        probs = jnp.exp(scores - log_total)
        dv_ref[0, :, columns] = unstacked(dot(probs.astype(jnp.bfloat16), grads)).astype(
            jnp.bfloat16
        )
        prob_grad = dot_t(stacked(kv[p, 0, 1]), grads)
        score_grad = (probs * (prob_grad - delta) * scale).astype(jnp.bfloat16)
        dk_ref[0, :, columns] = unstacked(dot(score_grad, queries)).astype(jnp.bfloat16)

    def gate_copy(r, step):
        target, digit, other = partner(r, step)
        return pltpu.make_async_remote_copy(
            src_ref=gbuf.at[r, digit],
            dst_ref=gbuf.at[r, digit],
            send_sem=g_send.at[r, step],
            recv_sem=g_recv.at[r, digit],
            device_id=target,
            device_id_type=MESH,
        )

    def gate_arrived(r, step):
        target, digit, other = partner(r, step)
        pltpu.make_async_remote_copy(
            src_ref=gbuf.at[r, digit],
            dst_ref=gbuf.at[r, other],
            send_sem=g_send.at[r, step],
            recv_sem=g_recv.at[r, other],
            device_id=target,
            device_id_type=MESH,
        ).wait_recv()

    def gate_total(r):
        for step in range(1, rounds[r][2]):
            gate_arrived(r, step)
        total = gbuf[r, 0]
        for i in range(1, rounds[r][2]):
            total = total + gbuf[r, i]
        return total

    def gate_send(r):
        block = gacc[...] if r == 0 else gate_total(r - 1)
        gbuf[r, partner(r, 0)[1]] = block
        for step in range(1, rounds[r][2]):
            gate_copy(r, step).start()

    def first_step(i, carry):
        @pl.when(i < pairs)
        def _():
            arrived(kv, kv_send, kv_recv, i, FROM_LOW2)
            arrived(kv, kv_send, kv_recv, i, FROM_HIGH2)
            block_copy(kv, kv_send, kv_recv, i, 3).start()

        @pl.when(i > 0)
        def _():
            arrived(kv, kv_send, kv_recv, i - 1, FROM_LOW1)
            arrived(kv, kv_send, kv_recv, i - 1, FROM_HIGH1)
            query_side(i - 1)

        return carry

    lax.fori_loop(0, pairs + 1, first_step, 0)

    def second_step(i, carry):
        for r in range(len(rounds)):

            @pl.when(i == r)
            def _():
                gate_send(r)

        @pl.when(i < pairs)
        def _():
            arrived(qg, qg_send, qg_recv, i, FROM_LOW2)
            arrived(qg, qg_send, qg_recv, i, FROM_HIGH2)
            block_copy(qg, qg_send, qg_recv, i, 3).start()

        @pl.when(i > 0)
        def _():
            for slot in (FROM_LOW1, FROM_HIGH1):
                arrived(qg, qg_send, qg_recv, i - 1, slot)
            for slot in range(1, 5):
                stat_copy(i - 1, slot).wait_recv()
            key_side(i - 1)

        return carry

    lax.fori_loop(0, pairs + 1, second_step, 0)

    total = gate_total(len(rounds) - 1)
    low_row = lax.broadcasted_iota(jnp.int32, total.shape, 1) < head_size
    sums_low = jnp.sum(jnp.where(low_row, total, 0.0), axis=1, keepdims=True)
    sums_high = jnp.sum(jnp.where(low_row, 0.0, total), axis=1, keepdims=True)
    place = lax.broadcasted_iota(jnp.int32, total.shape, 1)
    row = lax.broadcasted_iota(jnp.int32, total.shape, 0)
    spread = jnp.where(place == 2 * row, sums_low, 0.0) + jnp.where(
        place == 2 * row + 1, sums_high, 0.0
    )
    divisor = math.sqrt(n_view * n_seq * tokens * head_size)
    gg_ref[...] = jnp.sum(spread, axis=0, keepdims=True) * (1.0 / divisor)

    def drain(p, carry):
        for index in range(4):
            block_copy(kv, kv_send, kv_recv, p, index).wait_send()
            block_copy(qg, qg_send, qg_recv, p, index).wait_send()
        for slot in range(1, 5):
            stat_copy(p, slot).wait_send()
        return carry

    lax.fori_loop(0, pairs, drain, 0)
    for r in range(len(rounds)):
        for step in range(1, rounds[r][2]):
            gate_copy(r, step).wait_send()


def shards(query_rows, key_rows, value_rows, head_gate, cotangent, neighbours, counts):
    _, tokens, width = query_rows.shape
    heads = head_gate.shape[0]
    pairs = width // LANES
    n_view, n_seq = lax.axis_size("view"), lax.axis_size("seq")
    rounds = sum_rounds(n_view, n_seq)
    most = max(r[2] for r in rounds)
    smem = pl.BlockSpec(memory_space=pltpu.SMEM)
    vmem = pl.BlockSpec(memory_space=pltpu.VMEM)
    anywhere = pl.BlockSpec(memory_space=pl.ANY)
    rows = jax.ShapeDtypeStruct(query_rows.shape, jnp.bfloat16)
    dma = pltpu.SemaphoreType.DMA
    out, dq, dk, dv, gate = pl.pallas_call(
        functools.partial(kernel, (n_view, n_seq, pairs, width // heads)),
        out_shape=[rows] * 4 + [jax.ShapeDtypeStruct((1, LANES), jnp.float32)],
        in_specs=[smem] * 3 + [anywhere] * 4,
        out_specs=[vmem] * 5,
        scratch_shapes=[
            pltpu.VMEM((pairs, 5, 2, tokens, LANES), jnp.bfloat16),
            pltpu.VMEM((pairs, 5, 2, tokens, LANES), jnp.bfloat16),
            pltpu.VMEM((pairs, tokens, LANES), jnp.bfloat16),
            pltpu.VMEM((pairs, 5, 8, LANES), jnp.float32),
            pltpu.VMEM((8, LANES), jnp.float32),
            pltpu.VMEM((len(rounds), most, 8, LANES), jnp.float32),
            dma((pairs, 4)),
            dma((pairs, 4)),
            dma((pairs, 5)),
            dma((pairs, 4)),
            dma((pairs, 5)),
            dma((pairs, 5)),
            dma((pairs, 5)),
            dma((len(rounds), most)),
            dma((len(rounds), most)),
        ],
        compiler_params=pltpu.CompilerParams(
            collective_id=0, has_side_effects=True, vmem_limit_bytes=40 * 1024 * 1024
        ),
        cost_estimate=pl.CostEstimate(
            flops=2 * 8 * 5 * heads * tokens * tokens * 64, bytes_accessed=3200000, transcendentals=0
        ),
    )(head_gate, neighbours, counts, query_rows, key_rows, value_rows, cotangent)
    return out, dq, dk, dv, gate[0, :heads]


def solution(mesh):
    in_specs = (
        P("view", "seq", None),
        P("view", "seq", None),
        P("view", "seq", None),
        P(),
        P("view", "seq", None),
        P("view", None),
        P("view"),
    )
    out_specs = (
        P("view", "seq", None),
        P("view", "seq", None),
        P("view", "seq", None),
        P("view", "seq", None),
        P(),
    )
    return jax.shard_map(shards, mesh=mesh, in_specs=in_specs, out_specs=out_specs, check_vma=False)
```

```python
import functools
import math

import jax
import jax.numpy as jnp
from jax import lax
from jax.experimental import pallas as pl
from jax.experimental.pallas import tpu as pltpu
from jax.sharding import PartitionSpec as P

MESH = pl.DeviceIdType.MESH
LANES = 128
OFFSETS = (0, -2, -1, 1, 2)
FROM_LOW2, FROM_LOW1, FROM_HIGH1, FROM_HIGH2 = 1, 2, 3, 4
KEYS, QUERIES, STATS = 0, 1, 2


def sum_rounds(n_view, n_seq):
    high = math.gcd(n_view // 2, 4)
    low = math.gcd(n_seq, 4)
    groups = [
        [("view", 1, 2)],
        [("view", 2 * high, n_view // (2 * high))],
        [("seq", low, n_seq // low)],
        [("view", 2, high), ("seq", 1, low)],
    ]
    return [g for g in groups if group_size(g) > 1]


def group_size(group):
    return math.prod(size for _, _, size in group)


def kernel(
    sizes,
    counts_s, gate_hbm, neigh_hbm, q_hbm, k_hbm, v_hbm, c_hbm,
    out_ref, dq_ref, dk_ref, dv_ref, gg_ref,
    gate_s, neigh_s, kv, qg, cot, stats, gacc, gbuf,
    small_sem, load_sem, send_sem, recv_sem, g_send, g_recv,
):
    n_view, n_seq, pairs, head_size = sizes
    tokens = kv.shape[3]
    scale = 1.0 / math.sqrt(head_size)
    me = lax.axis_index("view")
    me_seq = lax.axis_index("seq")
    core = lax.rem(me, 2)
    sibling = me + 1 - 2 * core
    rounds = sum_rounds(n_view, n_seq)

    def view_at(offset):
        return lax.rem(me + offset + n_view, n_view)

    def partner(group, step):
        index = {"view": me, "seq": me_seq}
        place = 0
        for axis, stride, size in group:
            place = place * size + lax.rem(index[axis] // stride, size)
        other = lax.rem(place + step, group_size(group))
        target = {}
        rest = other
        for axis, stride, size in reversed(group):
            digit = lax.rem(index[axis] // stride, size)
            target[axis] = index[axis] + (lax.rem(rest, size) - digit) * stride
            rest = rest // size
        return target, place, other

    def load(hbm, column, p, dst):
        return pltpu.make_async_copy(
            hbm.at[0, :, pl.ds(p * LANES, LANES)], dst, load_sem.at[p, column]
        )

    loads = []
    for p in range(pairs):
        loads.append(
            [
                load(k_hbm, 0, p, kv.at[p, 0, 0]),
                load(v_hbm, 1, p, kv.at[p, 0, 1]),
                load(q_hbm, 2, p, qg.at[p, 0, 0]),
                load(c_hbm, 3, p, cot.at[p]),
            ]
        )
    for column in range(4):
        for p in range(pairs):
            loads[p][column].start()

    smalls = [
        pltpu.make_async_copy(src, dst, small_sem.at[i])
        for i, (src, dst) in enumerate(((gate_hbm, gate_s), (neigh_hbm, neigh_s)))
    ]
    for copy in smalls:
        copy.start()

    barrier = pltpu.get_barrier_semaphore()
    greeted = 0
    for offset in OFFSETS[1:]:
        pl.semaphore_signal(
            barrier, inc=1, device_id={"view": view_at(offset)}, device_id_type=MESH
        )
        greeted += 1
    for group in rounds:
        for step in range(1, group_size(group)):
            pl.semaphore_signal(
                barrier, inc=1, device_id=partner(group, step)[0], device_id_type=MESH
            )
            greeted += 1
    pl.semaphore_wait(barrier, greeted)

    def views(kind, p, slot):
        if kind is STATS:
            return stats.at[p, slot, pl.ds(0, 4)]
        return (kv if kind is KEYS else qg).at[p, slot]

    def block_copy(kind, p, index):
        src_slot, dst_slot, target = (
            (0, FROM_LOW2, view_at(2)),
            (0, FROM_HIGH2, view_at(-2)),
            (0, 2 + core, sibling),
            (4 - 3 * core, 3 - core, sibling),
        )[index]
        return pltpu.make_async_remote_copy(
            src_ref=views(kind, p, src_slot),
            dst_ref=views(kind, p, dst_slot),
            send_sem=send_sem.at[kind, p, index],
            recv_sem=recv_sem.at[kind, p, dst_slot],
            device_id={"view": target},
            device_id_type=MESH,
        )

    def send(kind, p):
        for index in range(3):
            block_copy(kind, p, index).start()

    def arrived(kind, p, slot):
        pltpu.make_async_remote_copy(
            src_ref=views(kind, p, 0),
            dst_ref=views(kind, p, slot),
            send_sem=send_sem.at[kind, p, 0],
            recv_sem=recv_sem.at[kind, p, slot],
            device_id={"view": sibling},
            device_id_type=MESH,
        ).wait_recv()

    def pass_on(kind, p):
        arrived(kind, p, FROM_LOW2)
        arrived(kind, p, FROM_HIGH2)
        block_copy(kind, p, 3).start()

    def chip_arrived(kind, p):
        arrived(kind, p, FROM_LOW1)
        arrived(kind, p, FROM_HIGH1)

    def sent(kind, p):
        for index in range(4):
            block_copy(kind, p, index).wait_send()

    for p in range(pairs):
        loads[p][0].wait()
        loads[p][1].wait()
        send(KEYS, p)
    for p in range(pairs):
        loads[p][2].wait()
        loads[p][3].wait()
    for copy in smalls:
        copy.wait()

    bias = [jnp.float32(0.0)]
    for offset in OFFSETS[1:]:
        view = view_at(offset)
        present = (neigh_s[0, 0] == view) & (counts_s[0] > 0)
        for j in range(1, 4):
            present = present | ((neigh_s[0, j] == view) & (counts_s[0] > j))
        bias.append(jnp.where(present, jnp.float32(0.0), jnp.float32(-jnp.inf)))
    bias_row = jnp.concatenate([jnp.full((1, tokens), b, jnp.float32) for b in bias], axis=1)
    lane = lax.broadcasted_iota(jnp.int32, (tokens, LANES), 1)
    low_half = lane < head_size

    def stacked(block):
        zero = jnp.zeros_like(block)
        return jnp.concatenate(
            [jnp.where(low_half, block, zero), jnp.where(low_half, zero, block)], axis=0
        )

    def unstacked(block):
        return jnp.where(low_half, block[:tokens], block[tokens:])

    def dot_t(a, b):
        return lax.dot_general(
            a, b, (((1,), (1,)), ((), ())), preferred_element_type=jnp.float32
        )

    def dot(a, b):
        return jnp.dot(a, b, preferred_element_type=jnp.float32)

    gacc[...] = jnp.zeros_like(gacc)

    def query_side(p):
        columns = pl.ds(pl.multiple_of(p * LANES, LANES), LANES)
        gate_row = jnp.where(low_half[:1], gate_s[2 * p], gate_s[2 * p + 1])
        cot_block = cot[p].astype(jnp.float32)
        grad = (gate_row * cot_block).astype(jnp.bfloat16)
        qg[p, 0, 1] = grad
        keys = kv[p, :, 0].reshape(5 * tokens, LANES)
        values = kv[p, :, 1].reshape(5 * tokens, LANES)
        scores = dot_t(stacked(qg[p, 0, 0]), keys) * scale + bias_row
        top = jnp.max(scores, axis=1, keepdims=True)
        raised = jnp.exp(scores - top)
        total = jnp.sum(raised, axis=1, keepdims=True)
        probs = raised * (1.0 / total)
        log_total = top + jnp.log(total)
        attended = unstacked(dot(probs.astype(jnp.bfloat16), values))
        out_ref[0, :, columns] = (gate_row * attended).astype(jnp.bfloat16)
        gacc[pl.ds(p, 1), :] = jnp.sum(cot_block * attended, axis=0, keepdims=True)
        product = grad.astype(jnp.float32) * attended
        delta_low = jnp.sum(jnp.where(low_half, product, 0.0), axis=1, keepdims=True)
        delta_high = jnp.sum(jnp.where(low_half, 0.0, product), axis=1, keepdims=True)
        table = jnp.where(lane == 0, log_total[:tokens], log_total[tokens:])
        table = jnp.where(lane == 2, delta_low, table)
        table = jnp.where(lane == 3, delta_high, table)
        stats[p, 0] = jnp.transpose(table)[:8]
        send(STATS, p)

        @pl.when(p < pairs - 1)
        def _():
            send(QUERIES, p)

        prob_grad = dot_t(stacked(grad), values)
        delta = jnp.concatenate([delta_low, delta_high], axis=0)
        score_grad = (probs * (prob_grad - delta) * scale).astype(jnp.bfloat16)
        dq_ref[0, :, columns] = unstacked(dot(score_grad, keys)).astype(jnp.bfloat16)

    def key_side(p):
        columns = pl.ds(pl.multiple_of(p * LANES, LANES), LANES)
        queries = qg[p, :, 0].reshape(5 * tokens, LANES)
        grads = qg[p, :, 1].reshape(5 * tokens, LANES)
        tables = [stats[p, slot] for slot in range(5)]
        rows = jnp.concatenate(tables, axis=1)

        def both(first, second):
            shape = (tokens, 5 * tokens)
            return jnp.concatenate(
                [jnp.broadcast_to(first, shape), jnp.broadcast_to(second, shape)], axis=0
            )

        log_total = both(rows[0:1] - bias_row, rows[1:2] - bias_row)
        delta = both(rows[2:3], rows[3:4])
        scores = dot_t(stacked(kv[p, 0, 0]), queries) * scale
        probs = jnp.exp(scores - log_total)
        dv_ref[0, :, columns] = unstacked(dot(probs.astype(jnp.bfloat16), grads)).astype(
            jnp.bfloat16
        )
        prob_grad = dot_t(stacked(kv[p, 0, 1]), grads)
        score_grad = (probs * (prob_grad - delta) * scale).astype(jnp.bfloat16)
        dk_ref[0, :, columns] = unstacked(dot(score_grad, queries)).astype(jnp.bfloat16)

    def gate_copy(r, step):
        target, place, _ = partner(rounds[r], step)
        row = gbuf.at[r, place, pl.ds(0, 1)]
        return pltpu.make_async_remote_copy(
            src_ref=row,
            dst_ref=row,
            send_sem=g_send.at[r, step],
            recv_sem=g_recv.at[r, place],
            device_id=target,
            device_id_type=MESH,
        )

    def gate_send(r, row):
        gbuf[r, partner(rounds[r], 0)[1], pl.ds(0, 1)] = row
        for step in range(1, group_size(rounds[r])):
            gate_copy(r, step).start()

    def gate_total(r):
        for step in range(1, group_size(rounds[r])):
            target, place, other = partner(rounds[r], step)
            pltpu.make_async_remote_copy(
                src_ref=gbuf.at[r, place, pl.ds(0, 1)],
                dst_ref=gbuf.at[r, other, pl.ds(0, 1)],
                send_sem=g_send.at[r, step],
                recv_sem=g_recv.at[r, other],
                device_id=target,
                device_id_type=MESH,
            ).wait_recv()
        total = gbuf[r, 0, pl.ds(0, 1)]
        for i in range(1, group_size(rounds[r])):
            total = total + gbuf[r, i, pl.ds(0, 1)]
        return total

    def first_step(i, carry):
        @pl.when(i < pairs)
        def _():
            pass_on(KEYS, i)

        @pl.when(i > 0)
        def _():
            chip_arrived(KEYS, i - 1)
            query_side(i - 1)

        return carry

    lax.fori_loop(0, pairs + 1, first_step, 0)

    sums = gacc[...]
    place = lax.broadcasted_iota(jnp.int32, sums.shape, 1)
    row = lax.broadcasted_iota(jnp.int32, sums.shape, 0)
    sums_low = jnp.sum(jnp.where(place < head_size, sums, 0.0), axis=1, keepdims=True)
    sums_high = jnp.sum(jnp.where(place < head_size, 0.0, sums), axis=1, keepdims=True)
    spread = jnp.where(place == 2 * row, sums_low, 0.0) + jnp.where(
        place == 2 * row + 1, sums_high, 0.0
    )
    gate_row = jnp.sum(spread, axis=0, keepdims=True)
    for r in range(len(rounds) - 1):
        gate_send(r, gate_row)
        gate_row = gate_total(r)
    gate_send(len(rounds) - 1, gate_row)
    send(QUERIES, pairs - 1)

    def second_step(i, carry):
        pass_on(STATS, i)
        pass_on(QUERIES, i)

        @pl.when(i > 0)
        def _():
            chip_arrived(STATS, i - 1)
            chip_arrived(QUERIES, i - 1)
            key_side(i - 1)
            sent(KEYS, i - 1)
            sent(STATS, i - 1)
            sent(QUERIES, i - 1)

        return carry

    last = pairs - 1
    lax.fori_loop(0, last, second_step, 0)
    chip_arrived(STATS, last - 1)
    chip_arrived(QUERIES, last - 1)
    key_side(last - 1)
    pass_on(STATS, last)
    divisor = math.sqrt(n_view * n_seq * tokens * head_size)
    gg_ref[...] = gate_total(len(rounds) - 1) * (1.0 / divisor)
    for r in range(len(rounds)):
        for step in range(1, group_size(rounds[r])):
            gate_copy(r, step).wait_send()
    sent(KEYS, last - 1)
    sent(STATS, last - 1)
    sent(QUERIES, last - 1)
    sent(KEYS, last)
    chip_arrived(STATS, last)
    sent(STATS, last)
    pass_on(QUERIES, last)
    chip_arrived(QUERIES, last)
    key_side(last)
    sent(QUERIES, last)


def hand_over(out, dq, dk, dv, gate, out_ref, dq_ref, dk_ref, dv_ref, gate_ref, sem):
    pairs = ((out, out_ref), (dq, dq_ref), (dk, dk_ref), (dv, dv_ref))
    copies = [pltpu.make_async_copy(a, b, sem.at[i]) for i, (a, b) in enumerate(pairs)]
    for copy in copies:
        copy.start()
    gate_ref[...] = gate[0, : gate_ref.shape[0]]
    for copy in copies:
        copy.wait()


def shards(query_rows, key_rows, value_rows, head_gate, cotangent, neighbours, counts):
    _, tokens, width = query_rows.shape
    heads = head_gate.shape[0]
    pairs = width // LANES
    n_view, n_seq = lax.axis_size("view"), lax.axis_size("seq")
    rounds = sum_rounds(n_view, n_seq)
    most = max(group_size(g) for g in rounds)
    vmem = pl.BlockSpec(memory_space=pltpu.VMEM)
    hbm = pl.BlockSpec(memory_space=pltpu.HBM)
    rows = jax.ShapeDtypeStruct(query_rows.shape, jnp.bfloat16)
    dma = pltpu.SemaphoreType.DMA
    operands = (head_gate, neighbours, query_rows, key_rows, value_rows, cotangent)
    results = pl.pallas_call(
        functools.partial(kernel, (n_view, n_seq, pairs, width // heads)),
        out_shape=[pltpu.VMEM(query_rows.shape, jnp.bfloat16)] * 4
        + [pltpu.VMEM((1, LANES), jnp.float32)],
        in_specs=[pl.BlockSpec(memory_space=pltpu.SMEM)] + [hbm] * 6,
        out_specs=[vmem] * 5,
        scratch_shapes=[
            pltpu.SMEM(head_gate.shape, jnp.float32),
            pltpu.SMEM(neighbours.shape, jnp.int32),
            pltpu.VMEM((pairs, 5, 2, tokens, LANES), jnp.bfloat16),
            pltpu.VMEM((pairs, 5, 2, tokens, LANES), jnp.bfloat16),
            pltpu.VMEM((pairs, tokens, LANES), jnp.bfloat16),
            pltpu.VMEM((pairs, 5, 8, LANES), jnp.float32),
            pltpu.VMEM((8, LANES), jnp.float32),
            pltpu.VMEM((len(rounds), most, 8, LANES), jnp.float32),
            dma((2,)),
            dma((pairs, 4)),
            dma((3, pairs, 4)),
            dma((3, pairs, 5)),
            dma((len(rounds), most)),
            dma((len(rounds), most)),
        ],
        compiler_params=pltpu.CompilerParams(
            collective_id=0, has_side_effects=True, vmem_limit_bytes=40 * 1024 * 1024
        ),
        cost_estimate=pl.CostEstimate(
            flops=2 * 8 * 5 * heads * tokens * tokens * 64, bytes_accessed=3200000, transcendentals=0
        ),
    )(counts, *(pltpu.with_memory_space_constraint(a, pltpu.HBM) for a in operands))
    return pl.pallas_call(
        hand_over,
        out_shape=[rows] * 4 + [jax.ShapeDtypeStruct((heads,), jnp.float32)],
        in_specs=[vmem] * 5,
        out_specs=[hbm] * 4 + [vmem],
        scratch_shapes=[dma((4,))],
    )(*(pltpu.with_memory_space_constraint(a, pltpu.VMEM) for a in results))


def solution(mesh):
    in_specs = (
        P("view", "seq", None),
        P("view", "seq", None),
        P("view", "seq", None),
        P(),
        P("view", "seq", None),
        P("view", None),
        P("view"),
    )
    out_specs = (
        P("view", "seq", None),
        P("view", "seq", None),
        P("view", "seq", None),
        P("view", "seq", None),
        P(),
    )
    return jax.shard_map(shards, mesh=mesh, in_specs=in_specs, out_specs=out_specs, check_vma=False)
```

```python
import functools
import math

import jax
import jax.numpy as jnp
from jax import lax
from jax.experimental import pallas as pl
from jax.experimental.pallas import tpu as pltpu
from jax.sharding import PartitionSpec as P

MESH = pl.DeviceIdType.MESH
LANES = 128
OFFSETS = (0, -2, -1, 1, 2)
FROM_LOW2, FROM_LOW1, FROM_HIGH1, FROM_HIGH2 = 1, 2, 3, 4
WINDOWS = (5, 3, 3, 5)
KEYS, QUERIES, STATS = 0, 1, 2


Z_STEPS = ((1, 2), (-1, -2), (2, 4))


def sum_groups(n_view, n_seq):
    high = math.gcd(n_view // 2, 4)
    low = math.gcd(n_seq, 4)
    free = [("view", 1, 2), ("view", 2 * high, n_view // (2 * high)), ("seq", low, n_seq // low)]
    return [g for g in free if g[2] > 1], ("seq", 1, low), ("view", 2, high)


def kernel(
    sizes,
    counts_s, gate_hbm, neigh_hbm, q_hbm, k_hbm, v_hbm, c_hbm,
    out_ref, dq_ref, dk_ref, dv_ref, gg_ref,
    gate_s, neigh_s, kv, qg, cot, stats, gacc, gbuf,
    small_sem, load_sem, send_sem, recv_sem, g_send, g_recv, far_sem, low_sem,
):
    n_view, n_seq, pairs, head_size = sizes
    tokens = kv.shape[3]
    scale = 1.0 / math.sqrt(head_size)
    me = lax.axis_index("view")
    me_seq = lax.axis_index("seq")
    core = lax.rem(me, 2)
    sibling = me + 1 - 2 * core
    free, z_lo, z_hi = sum_groups(n_view, n_seq)

    def view_at(offset):
        return lax.rem(me + offset + n_view, n_view)

    def digit_of(digit):
        axis, stride, size = digit
        return lax.rem((me if axis == "view" else me_seq) // stride, size)

    def partner(digit, step):
        axis, stride, size = digit
        here = digit_of(digit)
        there = lax.rem(here + step, size)
        return {axis: (me if axis == "view" else me_seq) + (there - here) * stride}, there

    barrier = pltpu.get_barrier_semaphore()
    greeted = 0
    for target in (view_at(2), view_at(-2), sibling):
        pl.semaphore_signal(
            barrier, inc=1, device_id={"view": target}, device_id_type=MESH
        )
        greeted += 1
    for digit in free + [z_lo]:
        for step in range(1, digit[2]):
            pl.semaphore_signal(
                barrier, inc=1, device_id=partner(digit, step)[0], device_id_type=MESH
            )
            greeted += 1

    def load(hbm, column, p, dst):
        return pltpu.make_async_copy(
            hbm.at[0, :, pl.ds(p * LANES, LANES)], dst, load_sem.at[p, column]
        )

    loads = []
    for p in range(pairs):
        loads.append(
            [
                load(k_hbm, 0, p, kv.at[p, 0, 0]),
                load(v_hbm, 1, p, kv.at[p, 0, 1]),
                load(q_hbm, 2, p, qg.at[p, 0, 0]),
                load(c_hbm, 3, p, cot.at[p]),
            ]
        )
    for column in range(4):
        for p in range(pairs):
            loads[p][column].start()

    smalls = [
        pltpu.make_async_copy(src, dst, small_sem.at[i])
        for i, (src, dst) in enumerate(((gate_hbm, gate_s), (neigh_hbm, neigh_s)))
    ]
    for copy in smalls:
        copy.start()

    pl.semaphore_wait(barrier, greeted)
    pl.semaphore_signal(
        far_sem, inc=1, device_id={"view": view_at(-2)}, device_id_type=MESH
    )

    def views(kind, p, slot):
        if kind is STATS:
            return stats.at[p, slot, pl.ds(0, 4)]
        return (kv if kind is KEYS else qg).at[p, slot]

    def block_copy(kind, p, index):
        src_slot, dst_slot, target = (
            (0, FROM_LOW2, view_at(2)),
            (0, FROM_HIGH2, view_at(-2)),
            (0, 2 + core, sibling),
            (4 - 3 * core, 3 - core, sibling),
        )[index]
        return pltpu.make_async_remote_copy(
            src_ref=views(kind, p, src_slot),
            dst_ref=views(kind, p, dst_slot),
            send_sem=send_sem.at[kind, p, index],
            recv_sem=recv_sem.at[kind, p, dst_slot],
            device_id={"view": target},
            device_id_type=MESH,
        )

    def send(kind, p):
        for index in range(3):
            block_copy(kind, p, index).start()

    def arrived(kind, p, slot):
        pltpu.make_async_remote_copy(
            src_ref=views(kind, p, 0),
            dst_ref=views(kind, p, slot),
            send_sem=send_sem.at[kind, p, 0],
            recv_sem=recv_sem.at[kind, p, slot],
            device_id={"view": sibling},
            device_id_type=MESH,
        ).wait_recv()

    def pass_on(kind, p):
        arrived(kind, p, 4 - 3 * core)
        block_copy(kind, p, 3).start()
        arrived(kind, p, 1 + 3 * core)

    def chip_arrived(kind, p):
        arrived(kind, p, FROM_LOW1)
        arrived(kind, p, FROM_HIGH1)

    def sent(kind, p):
        for index in range(4):
            block_copy(kind, p, index).wait_send()

    window = jnp.int32(WINDOWS[0])
    for place in range(1, len(WINDOWS)):
        here = lax.rem(me_seq, len(WINDOWS)) == place
        window = jnp.where(here, WINDOWS[place], window)

    for p in range(pairs):
        loads[p][0].wait()
        loads[p][1].wait()
        if p < min(WINDOWS):
            send(KEYS, p)
        elif p < max(WINDOWS):

            @pl.when(p < window)
            def _():
                send(KEYS, p)
        if p == 1:
            pl.semaphore_wait(far_sem, 1)
            for step in range(1, z_lo[2]):
                pl.semaphore_signal(
                    low_sem, inc=1, device_id=partner(z_lo, step)[0], device_id_type=MESH
                )
    for p in range(pairs):
        loads[p][2].wait()
        loads[p][3].wait()
    for copy in smalls:
        copy.wait()
    lane = lax.broadcasted_iota(jnp.int32, (tokens, LANES), 1)
    low_half = lane < head_size
    last = pairs - 1

    def gate_of(p):
        return jnp.where(low_half[:1], gate_s[2 * p], gate_s[2 * p + 1])

    for p in range(pairs):
        qg[p, 0, 1] = (gate_of(p) * cot[p].astype(jnp.float32)).astype(jnp.bfloat16)

    bias = [jnp.float32(0.0)]
    for offset in OFFSETS[1:]:
        view = view_at(offset)
        present = (neigh_s[0, 0] == view) & (counts_s[0] > 0)
        for j in range(1, 4):
            present = present | ((neigh_s[0, j] == view) & (counts_s[0] > j))
        bias.append(jnp.where(present, jnp.float32(0.0), jnp.float32(-jnp.inf)))
    bias_row = jnp.concatenate([jnp.full((1, tokens), b, jnp.float32) for b in bias], axis=1)

    def stacked(block):
        zero = jnp.zeros_like(block)
        return jnp.concatenate(
            [jnp.where(low_half, block, zero), jnp.where(low_half, zero, block)], axis=0
        )

    def unstacked(block):
        return jnp.where(low_half, block[:tokens], block[tokens:])

    def dot_t(a, b):
        return lax.dot_general(
            a, b, (((1,), (1,)), ((), ())), preferred_element_type=jnp.float32
        )

    def dot(a, b):
        return jnp.dot(a, b, preferred_element_type=jnp.float32)

    gacc[...] = jnp.zeros_like(gacc)

    def query_side(p):
        columns = pl.ds(pl.multiple_of(p * LANES, LANES), LANES)
        gate_row = gate_of(p)
        cot_block = cot[p].astype(jnp.float32)
        grad = qg[p, 0, 1]
        keys = kv[p, :, 0].reshape(5 * tokens, LANES)
        values = kv[p, :, 1].reshape(5 * tokens, LANES)
        scores = dot_t(stacked(qg[p, 0, 0]), keys) * scale + bias_row
        top = jnp.max(scores, axis=1, keepdims=True)
        raised = jnp.exp(scores - top)
        total = jnp.sum(raised, axis=1, keepdims=True)
        probs = raised * (1.0 / total)
        log_total = top + jnp.log(total)
        attended = unstacked(dot(probs.astype(jnp.bfloat16), values))
        out_ref[0, :, columns] = (gate_row * attended).astype(jnp.bfloat16)
        gacc[pl.ds(p, 1), :] = jnp.sum(cot_block * attended, axis=0, keepdims=True)
        product = grad.astype(jnp.float32) * attended
        delta_low = jnp.sum(jnp.where(low_half, product, 0.0), axis=1, keepdims=True)
        delta_high = jnp.sum(jnp.where(low_half, 0.0, product), axis=1, keepdims=True)
        table = jnp.where(lane == 0, log_total[:tokens], log_total[tokens:])
        table = jnp.where(lane == 2, delta_low, table)
        table = jnp.where(lane == 3, delta_high, table)
        stats[p, 0] = jnp.transpose(table)[:8]
        send(STATS, p)
        prob_grad = dot_t(stacked(grad), values)
        delta = jnp.concatenate([delta_low, delta_high], axis=0)
        score_grad = (probs * (prob_grad - delta) * scale).astype(jnp.bfloat16)
        dq_ref[0, :, columns] = unstacked(dot(score_grad, keys)).astype(jnp.bfloat16)

    def key_side(p):
        columns = pl.ds(pl.multiple_of(p * LANES, LANES), LANES)
        queries = qg[p, :, 0].reshape(5 * tokens, LANES)
        grads = qg[p, :, 1].reshape(5 * tokens, LANES)
        tables = [stats[p, slot] for slot in range(5)]
        rows = jnp.concatenate(tables, axis=1)

        def both(first, second):
            shape = (tokens, 5 * tokens)
            return jnp.concatenate(
                [jnp.broadcast_to(first, shape), jnp.broadcast_to(second, shape)], axis=0
            )

        log_total = both(rows[0:1] - bias_row, rows[1:2] - bias_row)
        delta = both(rows[2:3], rows[3:4])
        scores = dot_t(stacked(kv[p, 0, 0]), queries) * scale
        probs = jnp.exp(scores - log_total)
        dv_ref[0, :, columns] = unstacked(dot(probs.astype(jnp.bfloat16), grads)).astype(
            jnp.bfloat16
        )
        prob_grad = dot_t(stacked(kv[p, 0, 1]), grads)
        score_grad = (probs * (prob_grad - delta) * scale).astype(jnp.bfloat16)
        dk_ref[0, :, columns] = unstacked(dot(score_grad, queries)).astype(jnp.bfloat16)

    def gate_row(r, place):
        return gbuf.at[r, place, pl.ds(0, 1)]

    def gate_copy(r, step):
        target, _ = partner(free[r], step)
        place = digit_of(free[r])
        return pltpu.make_async_remote_copy(
            src_ref=gate_row(r, place),
            dst_ref=gate_row(r, place),
            send_sem=g_send.at[r, step],
            recv_sem=g_recv.at[r, place],
            device_id=target,
            device_id_type=MESH,
        )

    def gate_arrived(r, place):
        row = gate_row(r, place)
        pltpu.make_async_remote_copy(
            src_ref=row,
            dst_ref=row,
            send_sem=g_send.at[r, 0],
            recv_sem=g_recv.at[r, place],
            device_id={"view": sibling},
            device_id_type=MESH,
        ).wait_recv()

    def gate_total(r, size):
        total = gbuf[r, 0, pl.ds(0, 1)]
        for i in range(1, size):
            total = total + gbuf[r, i, pl.ds(0, 1)]
        return total

    def free_round(r, row):
        gbuf[r, digit_of(free[r]), pl.ds(0, 1)] = row
        for step in range(1, free[r][2]):
            gate_copy(r, step).start()
        for step in range(1, free[r][2]):
            gate_arrived(r, partner(free[r], step)[1])
        return gate_total(r, free[r][2])

    z_round = len(free)
    z_place = digit_of(z_hi) * z_lo[2] + digit_of(z_lo)

    def z_partners():
        for step_hi, distance in ((0, 0),) + Z_STEPS:
            for step in range(z_lo[2]):
                if distance or step:
                    target, low = partner(z_lo, step)
                    high = lax.rem(digit_of(z_hi) + step_hi + z_hi[2], z_hi[2])
                    yield {"view": view_at(distance), **target}, high * z_lo[2] + low

    def z_copies():
        for index, (target, _) in enumerate(z_partners()):
            yield pltpu.make_async_remote_copy(
                src_ref=gate_row(z_round, z_place),
                dst_ref=gate_row(z_round, z_place),
                send_sem=g_send.at[z_round, index],
                recv_sem=g_recv.at[z_round, z_place],
                device_id=target,
                device_id_type=MESH,
            )

    def send_later(i, base):
        low, high = base + min(WINDOWS), base + pairs + max(WINDOWS)
        for index in range(low, min(2 * pairs, high)):

            @pl.when(i + base == index - window)
            def _():
                send(index // pairs, index % pairs)

    def first_step(i, carry):
        @pl.when(i < pairs)
        def _():
            pass_on(KEYS, i)
            send_later(i, 0)

        @pl.when(i > 0)
        def _():
            chip_arrived(KEYS, i - 1)
            query_side(i - 1)

        return carry

    lax.fori_loop(0, pairs + 1, first_step, 0)

    sums = gacc[...]
    place = lax.broadcasted_iota(jnp.int32, sums.shape, 1)
    row = lax.broadcasted_iota(jnp.int32, sums.shape, 0)
    sums_low = jnp.sum(jnp.where(place < head_size, sums, 0.0), axis=1, keepdims=True)
    sums_high = jnp.sum(jnp.where(place < head_size, 0.0, sums), axis=1, keepdims=True)
    spread = jnp.where(place == 2 * row, sums_low, 0.0) + jnp.where(
        place == 2 * row + 1, sums_high, 0.0
    )
    row_sums = jnp.sum(spread, axis=0, keepdims=True)
    for r in range(len(free)):
        row_sums = free_round(r, row_sums)
    gbuf[z_round, z_place, pl.ds(0, 1)] = row_sums
    if z_lo[2] > 1:
        pl.semaphore_wait(low_sem, z_lo[2] - 1)
    for copy in z_copies():
        copy.start()

    def second_step(i, carry):
        pass_on(STATS, i)
        pass_on(QUERIES, i)
        send_later(i, pairs)

        @pl.when(i > 0)
        def _():
            chip_arrived(STATS, i - 1)
            chip_arrived(QUERIES, i - 1)
            key_side(i - 1)
            sent(KEYS, i - 1)
            sent(STATS, i - 1)
            sent(QUERIES, i - 1)

        return carry

    lax.fori_loop(0, last, second_step, 0)
    chip_arrived(STATS, last - 1)
    chip_arrived(QUERIES, last - 1)
    key_side(last - 1)
    pass_on(STATS, last)
    divisor = math.sqrt(n_view * n_seq * tokens * head_size)
    for _, place in z_partners():
        gate_arrived(z_round, place)
    gg_ref[...] = gate_total(z_round, z_hi[2] * z_lo[2]) * (1.0 / divisor)
    for r in range(len(free)):
        for step in range(1, free[r][2]):
            gate_copy(r, step).wait_send()
    for copy in z_copies():
        copy.wait_send()
    sent(KEYS, last - 1)
    sent(STATS, last - 1)
    sent(QUERIES, last - 1)
    sent(KEYS, last)
    chip_arrived(STATS, last)
    sent(STATS, last)
    pass_on(QUERIES, last)
    chip_arrived(QUERIES, last)
    key_side(last)
    sent(QUERIES, last)


def hand_over(out, dq, dk, dv, gate, out_ref, dq_ref, dk_ref, dv_ref, gate_ref, sem):
    pairs = ((out, out_ref), (dq, dq_ref), (dk, dk_ref), (dv, dv_ref))
    copies = [pltpu.make_async_copy(a, b, sem.at[i]) for i, (a, b) in enumerate(pairs)]
    for copy in copies:
        copy.start()
    gate_ref[...] = gate[0, : gate_ref.shape[0]]
    for copy in copies:
        copy.wait()


def shards(query_rows, key_rows, value_rows, head_gate, cotangent, neighbours, counts):
    _, tokens, width = query_rows.shape
    heads = head_gate.shape[0]
    pairs = width // LANES
    n_view, n_seq = lax.axis_size("view"), lax.axis_size("seq")
    free, z_lo, z_hi = sum_groups(n_view, n_seq)
    rounds, most = len(free) + 1, max(z_lo[2] * z_hi[2], *(digit[2] for digit in free))
    vmem = pl.BlockSpec(memory_space=pltpu.VMEM)
    hbm = pl.BlockSpec(memory_space=pltpu.HBM)
    rows = jax.ShapeDtypeStruct(query_rows.shape, jnp.bfloat16)
    dma = pltpu.SemaphoreType.DMA
    operands = (head_gate, neighbours, query_rows, key_rows, value_rows, cotangent)
    results = pl.pallas_call(
        functools.partial(kernel, (n_view, n_seq, pairs, width // heads)),
        out_shape=[pltpu.VMEM(query_rows.shape, jnp.bfloat16)] * 4
        + [pltpu.VMEM((1, LANES), jnp.float32)],
        in_specs=[pl.BlockSpec(memory_space=pltpu.SMEM)] + [hbm] * 6,
        out_specs=[vmem] * 5,
        scratch_shapes=[
            pltpu.SMEM(head_gate.shape, jnp.float32),
            pltpu.SMEM(neighbours.shape, jnp.int32),
            pltpu.VMEM((pairs, 5, 2, tokens, LANES), jnp.bfloat16),
            pltpu.VMEM((pairs, 5, 2, tokens, LANES), jnp.bfloat16),
            pltpu.VMEM((pairs, tokens, LANES), jnp.bfloat16),
            pltpu.VMEM((pairs, 5, 8, LANES), jnp.float32),
            pltpu.VMEM((8, LANES), jnp.float32),
            pltpu.VMEM((rounds, most, 8, LANES), jnp.float32),
            dma((2,)),
            dma((pairs, 4)),
            dma((3, pairs, 4)),
            dma((3, pairs, 5)),
            dma((rounds, most)),
            dma((rounds, most)),
            pltpu.SemaphoreType.REGULAR,
            pltpu.SemaphoreType.REGULAR,
        ],
        compiler_params=pltpu.CompilerParams(
            collective_id=0, has_side_effects=True, vmem_limit_bytes=40 * 1024 * 1024
        ),
        cost_estimate=pl.CostEstimate(
            flops=2 * 8 * 5 * heads * tokens * tokens * 64, bytes_accessed=3200000, transcendentals=0
        ),
    )(counts, *(pltpu.with_memory_space_constraint(a, pltpu.HBM) for a in operands))
    return pl.pallas_call(
        hand_over,
        out_shape=[rows] * 4 + [jax.ShapeDtypeStruct((heads,), jnp.float32)],
        in_specs=[vmem] * 5,
        out_specs=[hbm] * 4 + [vmem],
        scratch_shapes=[dma((4,))],
    )(*(pltpu.with_memory_space_constraint(a, pltpu.VMEM) for a in results))


def solution(mesh):
    in_specs = (
        P("view", "seq", None),
        P("view", "seq", None),
        P("view", "seq", None),
        P(),
        P("view", "seq", None),
        P("view", None),
        P("view"),
    )
    out_specs = (
        P("view", "seq", None),
        P("view", "seq", None),
        P("view", "seq", None),
        P("view", "seq", None),
        P(),
    )
    return jax.shard_map(shards, mesh=mesh, in_specs=in_specs, out_specs=out_specs, check_vma=False)
```

```python
import functools
import math

import jax
import jax.numpy as jnp
from jax import lax
from jax.experimental import pallas as pl
from jax.experimental.pallas import tpu as pltpu
from jax.sharding import PartitionSpec as P

MESH = pl.DeviceIdType.MESH
LANES = 128
OFFSETS = (0, -2, -1, 1, 2)
FROM_LOW2, FROM_LOW1, FROM_HIGH1, FROM_HIGH2 = 1, 2, 3, 4
WINDOWS = (5, 3, 4, 5)
KEYS, QUERIES, STATS = 0, 1, 2


Z_STEPS = ((1, 2), (-1, -2), (2, 4))


def sum_groups(n_view, n_seq):
    high = math.gcd(n_view // 2, 4)
    low = math.gcd(n_seq, 4)
    free = [("view", 1, 2), ("view", 2 * high, n_view // (2 * high)), ("seq", low, n_seq // low)]
    return [g for g in free if g[2] > 1], ("seq", 1, low), ("view", 2, high)


def kernel(
    sizes,
    counts_s, gate_hbm, neigh_hbm, q_hbm, k_hbm, v_hbm, c_hbm,
    out_ref, dq_ref, dk_ref, dv_ref, gg_ref,
    gate_s, neigh_s, kv, qg, cot, stats, gacc, gbuf,
    small_sem, load_sem, send_sem, recv_sem, g_send, g_recv, far_sem, low_sem,
):
    n_view, n_seq, pairs, head_size = sizes
    tokens = kv.shape[3]
    scale = 1.0 / math.sqrt(head_size)
    me = lax.axis_index("view")
    me_seq = lax.axis_index("seq")
    core = lax.rem(me, 2)
    sibling = me + 1 - 2 * core
    free, z_lo, z_hi = sum_groups(n_view, n_seq)

    def view_at(offset):
        return lax.rem(me + offset + n_view, n_view)

    def digit_of(digit):
        axis, stride, size = digit
        return lax.rem((me if axis == "view" else me_seq) // stride, size)

    def partner(digit, step):
        axis, stride, size = digit
        here = digit_of(digit)
        there = lax.rem(here + step, size)
        return {axis: (me if axis == "view" else me_seq) + (there - here) * stride}, there

    barrier = pltpu.get_barrier_semaphore()
    greeted = 0
    for target in (view_at(2), view_at(-2), sibling):
        pl.semaphore_signal(
            barrier, inc=1, device_id={"view": target}, device_id_type=MESH
        )
        greeted += 1
    for digit in free + [z_lo]:
        for step in range(1, digit[2]):
            pl.semaphore_signal(
                barrier, inc=1, device_id=partner(digit, step)[0], device_id_type=MESH
            )
            greeted += 1

    def load(hbm, column, p, dst):
        return pltpu.make_async_copy(
            hbm.at[0, :, pl.ds(p * LANES, LANES)], dst, load_sem.at[p, column]
        )

    loads = []
    for p in range(pairs):
        loads.append(
            [
                load(k_hbm, 0, p, kv.at[p, 0, 0]),
                load(v_hbm, 1, p, kv.at[p, 0, 1]),
                load(q_hbm, 2, p, qg.at[p, 0, 0]),
                load(c_hbm, 3, p, cot.at[p]),
            ]
        )
    for column in range(4):
        for p in range(pairs):
            loads[p][column].start()

    smalls = [
        pltpu.make_async_copy(src, dst, small_sem.at[i])
        for i, (src, dst) in enumerate(((gate_hbm, gate_s), (neigh_hbm, neigh_s)))
    ]
    for copy in smalls:
        copy.start()

    pl.semaphore_wait(barrier, greeted)
    pl.semaphore_signal(
        far_sem, inc=1, device_id={"view": view_at(-2)}, device_id_type=MESH
    )

    def views(kind, p, slot):
        if kind is STATS:
            return stats.at[p, slot, pl.ds(0, 4)]
        return (kv if kind is KEYS else qg).at[p, slot]

    def block_copy(kind, p, index):
        src_slot, dst_slot, target = (
            (0, FROM_LOW2, view_at(2)),
            (0, FROM_HIGH2, view_at(-2)),
            (0, 2 + core, sibling),
            (4 - 3 * core, 3 - core, sibling),
        )[index]
        return pltpu.make_async_remote_copy(
            src_ref=views(kind, p, src_slot),
            dst_ref=views(kind, p, dst_slot),
            send_sem=send_sem.at[kind, p, index],
            recv_sem=recv_sem.at[kind, p, dst_slot],
            device_id={"view": target},
            device_id_type=MESH,
        )

    def send(kind, p):
        for index in range(3):
            block_copy(kind, p, index).start()

    def arrived(kind, p, slot):
        pltpu.make_async_remote_copy(
            src_ref=views(kind, p, 0),
            dst_ref=views(kind, p, slot),
            send_sem=send_sem.at[kind, p, 0],
            recv_sem=recv_sem.at[kind, p, slot],
            device_id={"view": sibling},
            device_id_type=MESH,
        ).wait_recv()

    def pass_on(kind, p):
        arrived(kind, p, 4 - 3 * core)
        block_copy(kind, p, 3).start()
        arrived(kind, p, 1 + 3 * core)

    def chip_arrived(kind, p):
        arrived(kind, p, FROM_LOW1)
        arrived(kind, p, FROM_HIGH1)

    def sent(kind, p):
        for index in range(4):
            block_copy(kind, p, index).wait_send()

    window = jnp.int32(WINDOWS[0])
    for place in range(1, len(WINDOWS)):
        here = lax.rem(me_seq, len(WINDOWS)) == place
        window = jnp.where(here, WINDOWS[place], window)

    for p in range(pairs):
        loads[p][0].wait()
        loads[p][1].wait()
        if p < min(WINDOWS):
            send(KEYS, p)
        elif p < max(WINDOWS):

            @pl.when(p < window)
            def _():
                send(KEYS, p)
        if p == 1:
            pl.semaphore_wait(far_sem, 1)
            for step in range(1, z_lo[2]):
                pl.semaphore_signal(
                    low_sem, inc=1, device_id=partner(z_lo, step)[0], device_id_type=MESH
                )
    for p in range(pairs):
        loads[p][2].wait()
        loads[p][3].wait()
    for copy in smalls:
        copy.wait()
    lane = lax.broadcasted_iota(jnp.int32, (tokens, LANES), 1)
    low_half = lane < head_size
    last = pairs - 1

    def gate_of(p):
        return jnp.where(low_half[:1], gate_s[2 * p], gate_s[2 * p + 1])

    for p in range(pairs):
        qg[p, 0, 1] = (gate_of(p) * cot[p].astype(jnp.float32)).astype(jnp.bfloat16)

    bias = [jnp.float32(0.0)]
    for offset in OFFSETS[1:]:
        view = view_at(offset)
        present = (neigh_s[0, 0] == view) & (counts_s[0] > 0)
        for j in range(1, 4):
            present = present | ((neigh_s[0, j] == view) & (counts_s[0] > j))
        bias.append(jnp.where(present, jnp.float32(0.0), jnp.float32(-jnp.inf)))
    bias_row = jnp.concatenate([jnp.full((1, tokens), b, jnp.float32) for b in bias], axis=1)

    def stacked(block):
        zero = jnp.zeros_like(block)
        return jnp.concatenate(
            [jnp.where(low_half, block, zero), jnp.where(low_half, zero, block)], axis=0
        )

    def unstacked(block):
        return jnp.where(low_half, block[:tokens], block[tokens:])

    def dot_t(a, b):
        return lax.dot_general(
            a, b, (((1,), (1,)), ((), ())), preferred_element_type=jnp.float32
        )

    def dot(a, b):
        return jnp.dot(a, b, preferred_element_type=jnp.float32)

    gacc[...] = jnp.zeros_like(gacc)

    def query_side(p):
        columns = pl.ds(pl.multiple_of(p * LANES, LANES), LANES)
        gate_row = gate_of(p)
        cot_block = cot[p].astype(jnp.float32)
        grad = qg[p, 0, 1]
        keys = kv[p, :, 0].reshape(5 * tokens, LANES)
        values = kv[p, :, 1].reshape(5 * tokens, LANES)
        scores = dot_t(stacked(qg[p, 0, 0]), keys) * scale + bias_row
        top = jnp.max(scores, axis=1, keepdims=True)
        raised = jnp.exp(scores - top)
        total = jnp.sum(raised, axis=1, keepdims=True)
        probs = raised * (1.0 / total)
        log_total = top + jnp.log(total)
        attended = unstacked(dot(probs.astype(jnp.bfloat16), values))
        out_ref[0, :, columns] = (gate_row * attended).astype(jnp.bfloat16)
        gacc[pl.ds(p, 1), :] = jnp.sum(cot_block * attended, axis=0, keepdims=True)
        product = grad.astype(jnp.float32) * attended
        delta_low = jnp.sum(jnp.where(low_half, product, 0.0), axis=1, keepdims=True)
        delta_high = jnp.sum(jnp.where(low_half, 0.0, product), axis=1, keepdims=True)
        table = jnp.where(lane == 0, log_total[:tokens], log_total[tokens:])
        table = jnp.where(lane == 2, delta_low, table)
        table = jnp.where(lane == 3, delta_high, table)
        stats[p, 0] = jnp.transpose(table)[:8]
        send(STATS, p)
        prob_grad = dot_t(stacked(grad), values)
        delta = jnp.concatenate([delta_low, delta_high], axis=0)
        score_grad = (probs * (prob_grad - delta) * scale).astype(jnp.bfloat16)
        dq_ref[0, :, columns] = unstacked(dot(score_grad, keys)).astype(jnp.bfloat16)

    def key_side(p):
        columns = pl.ds(pl.multiple_of(p * LANES, LANES), LANES)
        queries = qg[p, :, 0].reshape(5 * tokens, LANES)
        grads = qg[p, :, 1].reshape(5 * tokens, LANES)
        tables = [stats[p, slot] for slot in range(5)]
        rows = jnp.concatenate(tables, axis=1)

        def both(first, second):
            shape = (tokens, 5 * tokens)
            return jnp.concatenate(
                [jnp.broadcast_to(first, shape), jnp.broadcast_to(second, shape)], axis=0
            )

        log_total = both(rows[0:1] - bias_row, rows[1:2] - bias_row)
        delta = both(rows[2:3], rows[3:4])
        scores = dot_t(stacked(kv[p, 0, 0]), queries) * scale
        probs = jnp.exp(scores - log_total)
        dv_ref[0, :, columns] = unstacked(dot(probs.astype(jnp.bfloat16), grads)).astype(
            jnp.bfloat16
        )
        prob_grad = dot_t(stacked(kv[p, 0, 1]), grads)
        score_grad = (probs * (prob_grad - delta) * scale).astype(jnp.bfloat16)
        dk_ref[0, :, columns] = unstacked(dot(score_grad, queries)).astype(jnp.bfloat16)

    def gate_row(r, place):
        return gbuf.at[r, place, pl.ds(0, 1)]

    def gate_copy(r, step):
        target, _ = partner(free[r], step)
        place = digit_of(free[r])
        return pltpu.make_async_remote_copy(
            src_ref=gate_row(r, place),
            dst_ref=gate_row(r, place),
            send_sem=g_send.at[r, step],
            recv_sem=g_recv.at[r, place],
            device_id=target,
            device_id_type=MESH,
        )

    def gate_arrived(r, place):
        row = gate_row(r, place)
        pltpu.make_async_remote_copy(
            src_ref=row,
            dst_ref=row,
            send_sem=g_send.at[r, 0],
            recv_sem=g_recv.at[r, place],
            device_id={"view": sibling},
            device_id_type=MESH,
        ).wait_recv()

    def gate_total(r, size):
        total = gbuf[r, 0, pl.ds(0, 1)]
        for i in range(1, size):
            total = total + gbuf[r, i, pl.ds(0, 1)]
        return total

    def free_round(r, row):
        gbuf[r, digit_of(free[r]), pl.ds(0, 1)] = row
        for step in range(1, free[r][2]):
            gate_copy(r, step).start()
        for step in range(1, free[r][2]):
            gate_arrived(r, partner(free[r], step)[1])
        return gate_total(r, free[r][2])

    z_round = len(free)
    z_place = digit_of(z_hi) * z_lo[2] + digit_of(z_lo)

    def z_partners():
        for step_hi, distance in ((0, 0),) + Z_STEPS:
            for step in range(z_lo[2]):
                if distance or step:
                    target, low = partner(z_lo, step)
                    high = lax.rem(digit_of(z_hi) + step_hi + z_hi[2], z_hi[2])
                    yield {"view": view_at(distance), **target}, high * z_lo[2] + low

    def z_copies():
        for index, (target, _) in enumerate(z_partners()):
            yield pltpu.make_async_remote_copy(
                src_ref=gate_row(z_round, z_place),
                dst_ref=gate_row(z_round, z_place),
                send_sem=g_send.at[z_round, index],
                recv_sem=g_recv.at[z_round, z_place],
                device_id=target,
                device_id_type=MESH,
            )

    def send_later(i, base):
        low, high = base + min(WINDOWS), base + pairs + max(WINDOWS)
        for index in range(low, min(2 * pairs, high)):

            @pl.when(i + base == index - window)
            def _():
                send(index // pairs, index % pairs)

    def first_step(i, carry):
        @pl.when(i < pairs)
        def _():
            pass_on(KEYS, i)
            send_later(i, 0)

        @pl.when(i > 0)
        def _():
            chip_arrived(KEYS, i - 1)
            query_side(i - 1)

        return carry

    lax.fori_loop(0, pairs + 1, first_step, 0)

    sums = gacc[...]
    place = lax.broadcasted_iota(jnp.int32, sums.shape, 1)
    row = lax.broadcasted_iota(jnp.int32, sums.shape, 0)
    sums_low = jnp.sum(jnp.where(place < head_size, sums, 0.0), axis=1, keepdims=True)
    sums_high = jnp.sum(jnp.where(place < head_size, 0.0, sums), axis=1, keepdims=True)
    spread = jnp.where(place == 2 * row, sums_low, 0.0) + jnp.where(
        place == 2 * row + 1, sums_high, 0.0
    )
    row_sums = jnp.sum(spread, axis=0, keepdims=True)
    for r in range(len(free)):
        row_sums = free_round(r, row_sums)
    gbuf[z_round, z_place, pl.ds(0, 1)] = row_sums
    if z_lo[2] > 1:
        pl.semaphore_wait(low_sem, z_lo[2] - 1)
    for copy in z_copies():
        copy.start()

    def second_step(i, carry):
        pass_on(STATS, i)
        pass_on(QUERIES, i)
        send_later(i, pairs)

        @pl.when(i > 0)
        def _():
            chip_arrived(STATS, i - 1)
            chip_arrived(QUERIES, i - 1)
            key_side(i - 1)
            sent(KEYS, i - 1)
            sent(STATS, i - 1)
            sent(QUERIES, i - 1)

        return carry

    lax.fori_loop(0, last, second_step, 0)
    chip_arrived(STATS, last - 1)
    chip_arrived(QUERIES, last - 1)
    key_side(last - 1)
    pass_on(STATS, last)
    sent(KEYS, last - 1)
    sent(STATS, last - 1)
    sent(QUERIES, last - 1)
    sent(KEYS, last)
    chip_arrived(STATS, last)
    sent(STATS, last)
    for r in range(len(free)):
        for step in range(1, free[r][2]):
            gate_copy(r, step).wait_send()
    pass_on(QUERIES, last)
    divisor = math.sqrt(n_view * n_seq * tokens * head_size)
    for _, place in z_partners():
        gate_arrived(z_round, place)
    gg_ref[...] = gate_total(z_round, z_hi[2] * z_lo[2]) * (1.0 / divisor)
    chip_arrived(QUERIES, last)
    key_side(last)
    for copy in z_copies():
        copy.wait_send()
    sent(QUERIES, last)


def hand_over(out, dq, dk, dv, gate, out_ref, dq_ref, dk_ref, dv_ref, gate_ref, sem):
    pairs = ((out, out_ref), (dq, dq_ref), (dk, dk_ref), (dv, dv_ref))
    copies = [pltpu.make_async_copy(a, b, sem.at[i]) for i, (a, b) in enumerate(pairs)]
    for copy in copies:
        copy.start()
    gate_ref[...] = gate[0, : gate_ref.shape[0]]
    for copy in copies:
        copy.wait()


def shards(query_rows, key_rows, value_rows, head_gate, cotangent, neighbours, counts):
    _, tokens, width = query_rows.shape
    heads = head_gate.shape[0]
    pairs = width // LANES
    n_view, n_seq = lax.axis_size("view"), lax.axis_size("seq")
    free, z_lo, z_hi = sum_groups(n_view, n_seq)
    rounds, most = len(free) + 1, max(z_lo[2] * z_hi[2], *(digit[2] for digit in free))
    vmem = pl.BlockSpec(memory_space=pltpu.VMEM)
    hbm = pl.BlockSpec(memory_space=pltpu.HBM)
    rows = jax.ShapeDtypeStruct(query_rows.shape, jnp.bfloat16)
    dma = pltpu.SemaphoreType.DMA
    operands = (head_gate, neighbours, query_rows, key_rows, value_rows, cotangent)
    results = pl.pallas_call(
        functools.partial(kernel, (n_view, n_seq, pairs, width // heads)),
        out_shape=[pltpu.VMEM(query_rows.shape, jnp.bfloat16)] * 4
        + [pltpu.VMEM((1, LANES), jnp.float32)],
        in_specs=[pl.BlockSpec(memory_space=pltpu.SMEM)] + [hbm] * 6,
        out_specs=[vmem] * 5,
        scratch_shapes=[
            pltpu.SMEM(head_gate.shape, jnp.float32),
            pltpu.SMEM(neighbours.shape, jnp.int32),
            pltpu.VMEM((pairs, 5, 2, tokens, LANES), jnp.bfloat16),
            pltpu.VMEM((pairs, 5, 2, tokens, LANES), jnp.bfloat16),
            pltpu.VMEM((pairs, tokens, LANES), jnp.bfloat16),
            pltpu.VMEM((pairs, 5, 8, LANES), jnp.float32),
            pltpu.VMEM((8, LANES), jnp.float32),
            pltpu.VMEM((rounds, most, 8, LANES), jnp.float32),
            dma((2,)),
            dma((pairs, 4)),
            dma((3, pairs, 4)),
            dma((3, pairs, 5)),
            dma((rounds, most)),
            dma((rounds, most)),
            pltpu.SemaphoreType.REGULAR,
            pltpu.SemaphoreType.REGULAR,
        ],
        compiler_params=pltpu.CompilerParams(
            collective_id=0, has_side_effects=True, vmem_limit_bytes=40 * 1024 * 1024
        ),
        cost_estimate=pl.CostEstimate(
            flops=2 * 8 * 5 * heads * tokens * tokens * 64, bytes_accessed=3200000, transcendentals=0
        ),
    )(counts, *(pltpu.with_memory_space_constraint(a, pltpu.HBM) for a in operands))
    return pl.pallas_call(
        hand_over,
        out_shape=[rows] * 4 + [jax.ShapeDtypeStruct((heads,), jnp.float32)],
        in_specs=[vmem] * 5,
        out_specs=[hbm] * 4 + [vmem],
        scratch_shapes=[dma((4,))],
    )(*(pltpu.with_memory_space_constraint(a, pltpu.VMEM) for a in results))


def solution(mesh):
    in_specs = (
        P("view", "seq", None),
        P("view", "seq", None),
        P("view", "seq", None),
        P(),
        P("view", "seq", None),
        P("view", None),
        P("view"),
    )
    out_specs = (
        P("view", "seq", None),
        P("view", "seq", None),
        P("view", "seq", None),
        P("view", "seq", None),
        P(),
    )
    return jax.shard_map(shards, mesh=mesh, in_specs=in_specs, out_specs=out_specs, check_vma=False)
```

```python
import functools
import math

import jax
import jax.numpy as jnp
from jax import lax
from jax.experimental import pallas as pl
from jax.experimental.pallas import tpu as pltpu
from jax.sharding import PartitionSpec as P

MESH = pl.DeviceIdType.MESH
LANES = 128
OFFSETS = (0, -2, -1, 1, 2)
FROM_LOW2, FROM_LOW1, FROM_HIGH1, FROM_HIGH2 = 1, 2, 3, 4
WINDOWS = (5, 3, 4, 5)
KEYS, QUERIES, STATS = 0, 1, 2


Z_STEPS = ((1, 2), (-1, -2), (2, 4))


def sum_groups(n_view, n_seq):
    high = math.gcd(n_view // 2, 4)
    low = math.gcd(n_seq, 4)
    free = [("view", 1, 2), ("view", 2 * high, n_view // (2 * high)), ("seq", low, n_seq // low)]
    return [g for g in free if g[2] > 1], ("seq", 1, low), ("view", 2, high)


def kernel(
    sizes,
    counts_s, gate_hbm, neigh_hbm, q_hbm, k_hbm, v_hbm, c_hbm,
    out_ref, dq_ref, dk_ref, dv_ref, gg_ref,
    gate_s, neigh_s, kv, qg, cot, stats, gacc, gbuf,
    small_sem, load_sem, send_sem, recv_sem, g_send, g_recv, far_sem, low_sem,
):
    n_view, n_seq, pairs, head_size = sizes
    tokens = kv.shape[3]
    scale = 1.0 / math.sqrt(head_size)
    me = lax.axis_index("view")
    me_seq = lax.axis_index("seq")
    core = lax.rem(me, 2)
    sibling = me + 1 - 2 * core
    free, z_lo, z_hi = sum_groups(n_view, n_seq)

    def view_at(offset):
        return lax.rem(me + offset + n_view, n_view)

    def digit_of(digit):
        axis, stride, size = digit
        return lax.rem((me if axis == "view" else me_seq) // stride, size)

    def partner(digit, step):
        axis, stride, size = digit
        here = digit_of(digit)
        there = lax.rem(here + step, size)
        return {axis: (me if axis == "view" else me_seq) + (there - here) * stride}, there

    barrier = pltpu.get_barrier_semaphore()
    greeted = 0
    for target in (view_at(2), view_at(-2), sibling):
        pl.semaphore_signal(
            barrier, inc=1, device_id={"view": target}, device_id_type=MESH
        )
        greeted += 1
    for digit in free + [z_lo]:
        for step in range(1, digit[2]):
            pl.semaphore_signal(
                barrier, inc=1, device_id=partner(digit, step)[0], device_id_type=MESH
            )
            greeted += 1

    def load(hbm, column, p, dst):
        return pltpu.make_async_copy(
            hbm.at[0, :, pl.ds(p * LANES, LANES)], dst, load_sem.at[p, column]
        )

    loads = []
    for p in range(pairs):
        loads.append(
            [
                load(k_hbm, 0, p, kv.at[p, 0, 0]),
                load(v_hbm, 1, p, kv.at[p, 0, 1]),
                load(q_hbm, 2, p, qg.at[p, 0, 0]),
                load(c_hbm, 3, p, cot.at[p]),
            ]
        )
    for column in range(4):
        for p in range(pairs):
            loads[p][column].start()

    smalls = [
        pltpu.make_async_copy(src, dst, small_sem.at[i])
        for i, (src, dst) in enumerate(((gate_hbm, gate_s), (neigh_hbm, neigh_s)))
    ]
    for copy in smalls:
        copy.start()

    pl.semaphore_wait(barrier, greeted)
    pl.semaphore_signal(
        far_sem, inc=1, device_id={"view": view_at(-2)}, device_id_type=MESH
    )

    def views(kind, p, slot):
        if kind is STATS:
            return stats.at[p, slot]
        return (kv if kind is KEYS else qg).at[p, slot]

    def block_copy(kind, p, index):
        src_slot, dst_slot, target = (
            (0, FROM_LOW2, view_at(2)),
            (0, FROM_HIGH2, view_at(-2)),
            (0, 2 + core, sibling),
            (4 - 3 * core, 3 - core, sibling),
        )[index]
        return pltpu.make_async_remote_copy(
            src_ref=views(kind, p, src_slot),
            dst_ref=views(kind, p, dst_slot),
            send_sem=send_sem.at[kind, p, index],
            recv_sem=recv_sem.at[kind, p, dst_slot],
            device_id={"view": target},
            device_id_type=MESH,
        )

    def send(kind, p):
        for index in range(3):
            block_copy(kind, p, index).start()

    def arrived(kind, p, slot):
        pltpu.make_async_remote_copy(
            src_ref=views(kind, p, 0),
            dst_ref=views(kind, p, slot),
            send_sem=send_sem.at[kind, p, 0],
            recv_sem=recv_sem.at[kind, p, slot],
            device_id={"view": sibling},
            device_id_type=MESH,
        ).wait_recv()

    def pass_on(kind, p):
        arrived(kind, p, 4 - 3 * core)
        block_copy(kind, p, 3).start()
        arrived(kind, p, 1 + 3 * core)

    def chip_arrived(kind, p):
        arrived(kind, p, FROM_LOW1)
        arrived(kind, p, FROM_HIGH1)

    def sent(kind, p):
        for index in range(4):
            block_copy(kind, p, index).wait_send()

    window = jnp.int32(WINDOWS[0])
    for place in range(1, len(WINDOWS)):
        here = lax.rem(me_seq, len(WINDOWS)) == place
        window = jnp.where(here, WINDOWS[place], window)

    for p in range(pairs):
        loads[p][0].wait()
        loads[p][1].wait()
        if p < min(WINDOWS):
            send(KEYS, p)
        elif p < max(WINDOWS):

            @pl.when(p < window)
            def _():
                send(KEYS, p)
        if p == 1:
            pl.semaphore_wait(far_sem, 1)
            for step in range(1, z_lo[2]):
                pl.semaphore_signal(
                    low_sem, inc=1, device_id=partner(z_lo, step)[0], device_id_type=MESH
                )
    for p in range(pairs):
        loads[p][2].wait()
        loads[p][3].wait()
    for copy in smalls:
        copy.wait()
    lane = lax.broadcasted_iota(jnp.int32, (tokens, LANES), 1)
    low_half = lane < head_size
    last = pairs - 1

    def gate_of(p):
        return jnp.where(low_half[:1], gate_s[2 * p], gate_s[2 * p + 1])

    for p in range(pairs):
        qg[p, 0, 1] = (gate_of(p) * cot[p].astype(jnp.float32)).astype(jnp.bfloat16)

    bias = [jnp.float32(0.0)]
    for offset in OFFSETS[1:]:
        view = view_at(offset)
        present = (neigh_s[0, 0] == view) & (counts_s[0] > 0)
        for j in range(1, 4):
            present = present | ((neigh_s[0, j] == view) & (counts_s[0] > j))
        bias.append(jnp.where(present, jnp.float32(0.0), jnp.float32(-jnp.inf)))
    bias_row = jnp.concatenate([jnp.full((1, tokens), b, jnp.float32) for b in bias], axis=1)

    def stacked(block):
        zero = jnp.zeros_like(block)
        return jnp.concatenate(
            [jnp.where(low_half, block, zero), jnp.where(low_half, zero, block)], axis=0
        )

    def unstacked(block):
        return jnp.where(low_half, block[:tokens], block[tokens:])

    def dot_t(a, b):
        return lax.dot_general(
            a, b, (((1,), (1,)), ((), ())), preferred_element_type=jnp.float32
        )

    def dot(a, b):
        return jnp.dot(a, b, preferred_element_type=jnp.float32)

    gacc[...] = jnp.zeros_like(gacc)

    def query_side(p):
        columns = pl.ds(pl.multiple_of(p * LANES, LANES), LANES)
        gate_row = gate_of(p)
        cot_block = cot[p].astype(jnp.float32)
        grad = qg[p, 0, 1]
        keys = kv[p, :, 0].reshape(5 * tokens, LANES)
        values = kv[p, :, 1].reshape(5 * tokens, LANES)
        scores = dot_t(stacked(qg[p, 0, 0]), keys) * scale + bias_row
        top = jnp.max(scores, axis=1, keepdims=True)
        raised = jnp.exp(scores - top)
        total = jnp.sum(raised, axis=1, keepdims=True)
        probs = raised * (1.0 / total)
        log_total = top + jnp.log(total)
        attended = unstacked(dot(probs.astype(jnp.bfloat16), values))
        out_ref[0, :, columns] = (gate_row * attended).astype(jnp.bfloat16)
        gacc[pl.ds(p, 1), :] = jnp.sum(cot_block * attended, axis=0, keepdims=True)
        product = grad.astype(jnp.float32) * attended
        delta_low = jnp.sum(jnp.where(low_half, product, 0.0), axis=1, keepdims=True)
        delta_high = jnp.sum(jnp.where(low_half, 0.0, product), axis=1, keepdims=True)
        table = jnp.where(lane == 0, log_total[:tokens], log_total[tokens:])
        table = jnp.where(lane == 2, delta_low, table)
        table = jnp.where(lane == 3, delta_high, table)
        stats[p // 2, 0, pl.ds(pl.multiple_of(lax.rem(p, 2) * 4, 4), 4)] = jnp.transpose(table)[:4]

        @pl.when(lax.rem(p, 2) == 1)
        def _():
            send(STATS, p // 2)

        prob_grad = dot_t(stacked(grad), values)
        delta = jnp.concatenate([delta_low, delta_high], axis=0)
        score_grad = (probs * (prob_grad - delta) * scale).astype(jnp.bfloat16)
        dq_ref[0, :, columns] = unstacked(dot(score_grad, keys)).astype(jnp.bfloat16)

    def key_side(p):
        columns = pl.ds(pl.multiple_of(p * LANES, LANES), LANES)
        queries = qg[p, :, 0].reshape(5 * tokens, LANES)
        grads = qg[p, :, 1].reshape(5 * tokens, LANES)
        tables = [stats[p // 2, slot] for slot in range(5)]
        both_rows = jnp.concatenate(tables, axis=1)
        rows = jnp.where(p % 2 == 0, both_rows[:4], both_rows[4:])

        def both(first, second):
            shape = (tokens, 5 * tokens)
            return jnp.concatenate(
                [jnp.broadcast_to(first, shape), jnp.broadcast_to(second, shape)], axis=0
            )

        log_total = both(rows[0:1] - bias_row, rows[1:2] - bias_row)
        delta = both(rows[2:3], rows[3:4])
        scores = dot_t(stacked(kv[p, 0, 0]), queries) * scale
        probs = jnp.exp(scores - log_total)
        dv_ref[0, :, columns] = unstacked(dot(probs.astype(jnp.bfloat16), grads)).astype(
            jnp.bfloat16
        )
        prob_grad = dot_t(stacked(kv[p, 0, 1]), grads)
        score_grad = (probs * (prob_grad - delta) * scale).astype(jnp.bfloat16)
        dk_ref[0, :, columns] = unstacked(dot(score_grad, queries)).astype(jnp.bfloat16)

    def gate_row(r, place):
        return gbuf.at[r, place, pl.ds(0, 1)]

    def gate_copy(r, step):
        target, _ = partner(free[r], step)
        place = digit_of(free[r])
        return pltpu.make_async_remote_copy(
            src_ref=gate_row(r, place),
            dst_ref=gate_row(r, place),
            send_sem=g_send.at[r, step],
            recv_sem=g_recv.at[r, place],
            device_id=target,
            device_id_type=MESH,
        )

    def gate_arrived(r, place):
        row = gate_row(r, place)
        pltpu.make_async_remote_copy(
            src_ref=row,
            dst_ref=row,
            send_sem=g_send.at[r, 0],
            recv_sem=g_recv.at[r, place],
            device_id={"view": sibling},
            device_id_type=MESH,
        ).wait_recv()

    def gate_total(r, size):
        total = gbuf[r, 0, pl.ds(0, 1)]
        for i in range(1, size):
            total = total + gbuf[r, i, pl.ds(0, 1)]
        return total

    def free_round(r, row):
        gbuf[r, digit_of(free[r]), pl.ds(0, 1)] = row
        for step in range(1, free[r][2]):
            gate_copy(r, step).start()
        for step in range(1, free[r][2]):
            gate_arrived(r, partner(free[r], step)[1])
        return gate_total(r, free[r][2])

    z_round = len(free)
    z_place = digit_of(z_hi) * z_lo[2] + digit_of(z_lo)

    def z_partners():
        for step_hi, distance in ((0, 0),) + Z_STEPS:
            for step in range(z_lo[2]):
                if distance or step:
                    target, low = partner(z_lo, step)
                    high = lax.rem(digit_of(z_hi) + step_hi + z_hi[2], z_hi[2])
                    yield {"view": view_at(distance), **target}, high * z_lo[2] + low

    def z_copies():
        for index, (target, _) in enumerate(z_partners()):
            yield pltpu.make_async_remote_copy(
                src_ref=gate_row(z_round, z_place),
                dst_ref=gate_row(z_round, z_place),
                send_sem=g_send.at[z_round, index],
                recv_sem=g_recv.at[z_round, z_place],
                device_id=target,
                device_id_type=MESH,
            )

    def send_later(i, base):
        low, high = base + min(WINDOWS), base + pairs + max(WINDOWS)
        for index in range(low, min(2 * pairs, high)):

            @pl.when(i + base == index - window)
            def _():
                send(index // pairs, index % pairs)

    def first_step(i, carry):
        @pl.when(i < pairs)
        def _():
            pass_on(KEYS, i)
            send_later(i, 0)

        @pl.when(i > 0)
        def _():
            chip_arrived(KEYS, i - 1)
            query_side(i - 1)

        return carry

    lax.fori_loop(0, pairs + 1, first_step, 0)

    sums = gacc[...]
    place = lax.broadcasted_iota(jnp.int32, sums.shape, 1)
    row = lax.broadcasted_iota(jnp.int32, sums.shape, 0)
    sums_low = jnp.sum(jnp.where(place < head_size, sums, 0.0), axis=1, keepdims=True)
    sums_high = jnp.sum(jnp.where(place < head_size, 0.0, sums), axis=1, keepdims=True)
    spread = jnp.where(place == 2 * row, sums_low, 0.0) + jnp.where(
        place == 2 * row + 1, sums_high, 0.0
    )
    row_sums = jnp.sum(spread, axis=0, keepdims=True)
    for r in range(len(free)):
        row_sums = free_round(r, row_sums)
    gbuf[z_round, z_place, pl.ds(0, 1)] = row_sums
    if z_lo[2] > 1:
        pl.semaphore_wait(low_sem, z_lo[2] - 1)
    for copy in z_copies():
        copy.start()

    def second_step(i, carry):
        @pl.when(lax.rem(i, 2) == 0)
        def _():
            pass_on(STATS, i // 2)

        pass_on(QUERIES, i)
        send_later(i, pairs)

        @pl.when(i > 0)
        def _():
            @pl.when(lax.rem(i, 2) == 1)
            def _():
                chip_arrived(STATS, i // 2)

            chip_arrived(QUERIES, i - 1)
            key_side(i - 1)
            sent(KEYS, i - 1)
            sent(QUERIES, i - 1)

        return carry

    lax.fori_loop(0, last, second_step, 0)
    chip_arrived(STATS, last // 2)
    chip_arrived(QUERIES, last - 1)
    key_side(last - 1)
    sent(KEYS, last - 1)
    sent(QUERIES, last - 1)
    sent(KEYS, last)
    for p in range(pairs // 2):
        sent(STATS, p)
    for r in range(len(free)):
        for step in range(1, free[r][2]):
            gate_copy(r, step).wait_send()
    pass_on(QUERIES, last)
    divisor = math.sqrt(n_view * n_seq * tokens * head_size)
    for _, place in z_partners():
        gate_arrived(z_round, place)
    gg_ref[...] = gate_total(z_round, z_hi[2] * z_lo[2]) * (1.0 / divisor)
    chip_arrived(QUERIES, last)
    key_side(last)
    for copy in z_copies():
        copy.wait_send()
    sent(QUERIES, last)


def hand_over(out, dq, dk, dv, gate, out_ref, dq_ref, dk_ref, dv_ref, gate_ref, sem):
    pairs = ((out, out_ref), (dq, dq_ref), (dk, dk_ref), (dv, dv_ref))
    copies = [pltpu.make_async_copy(a, b, sem.at[i]) for i, (a, b) in enumerate(pairs)]
    for copy in copies:
        copy.start()
    gate_ref[...] = gate[0, : gate_ref.shape[0]]
    for copy in copies:
        copy.wait()


def shards(query_rows, key_rows, value_rows, head_gate, cotangent, neighbours, counts):
    _, tokens, width = query_rows.shape
    heads = head_gate.shape[0]
    pairs = width // LANES
    n_view, n_seq = lax.axis_size("view"), lax.axis_size("seq")
    free, z_lo, z_hi = sum_groups(n_view, n_seq)
    rounds, most = len(free) + 1, max(z_lo[2] * z_hi[2], *(digit[2] for digit in free))
    vmem = pl.BlockSpec(memory_space=pltpu.VMEM)
    hbm = pl.BlockSpec(memory_space=pltpu.HBM)
    rows = jax.ShapeDtypeStruct(query_rows.shape, jnp.bfloat16)
    dma = pltpu.SemaphoreType.DMA
    operands = (head_gate, neighbours, query_rows, key_rows, value_rows, cotangent)
    results = pl.pallas_call(
        functools.partial(kernel, (n_view, n_seq, pairs, width // heads)),
        out_shape=[pltpu.VMEM(query_rows.shape, jnp.bfloat16)] * 4
        + [pltpu.VMEM((1, LANES), jnp.float32)],
        in_specs=[pl.BlockSpec(memory_space=pltpu.SMEM)] + [hbm] * 6,
        out_specs=[vmem] * 5,
        scratch_shapes=[
            pltpu.SMEM(head_gate.shape, jnp.float32),
            pltpu.SMEM(neighbours.shape, jnp.int32),
            pltpu.VMEM((pairs, 5, 2, tokens, LANES), jnp.bfloat16),
            pltpu.VMEM((pairs, 5, 2, tokens, LANES), jnp.bfloat16),
            pltpu.VMEM((pairs, tokens, LANES), jnp.bfloat16),
            pltpu.VMEM((pairs // 2, 5, 8, LANES), jnp.float32),
            pltpu.VMEM((8, LANES), jnp.float32),
            pltpu.VMEM((rounds, most, 8, LANES), jnp.float32),
            dma((2,)),
            dma((pairs, 4)),
            dma((3, pairs, 4)),
            dma((3, pairs, 5)),
            dma((rounds, most)),
            dma((rounds, most)),
            pltpu.SemaphoreType.REGULAR,
            pltpu.SemaphoreType.REGULAR,
        ],
        compiler_params=pltpu.CompilerParams(
            collective_id=0, has_side_effects=True, vmem_limit_bytes=40 * 1024 * 1024
        ),
        cost_estimate=pl.CostEstimate(
            flops=2 * 8 * 5 * heads * tokens * tokens * 64, bytes_accessed=3200000, transcendentals=0
        ),
    )(counts, *(pltpu.with_memory_space_constraint(a, pltpu.HBM) for a in operands))
    return pl.pallas_call(
        hand_over,
        out_shape=[rows] * 4 + [jax.ShapeDtypeStruct((heads,), jnp.float32)],
        in_specs=[vmem] * 5,
        out_specs=[hbm] * 4 + [vmem],
        scratch_shapes=[dma((4,))],
    )(*(pltpu.with_memory_space_constraint(a, pltpu.VMEM) for a in results))


def solution(mesh):
    in_specs = (
        P("view", "seq", None),
        P("view", "seq", None),
        P("view", "seq", None),
        P(),
        P("view", "seq", None),
        P("view", None),
        P("view"),
    )
    out_specs = (
        P("view", "seq", None),
        P("view", "seq", None),
        P("view", "seq", None),
        P("view", "seq", None),
        P(),
    )
    return jax.shard_map(shards, mesh=mesh, in_specs=in_specs, out_specs=out_specs, check_vma=False)
```
